32 devices in a mesh: pipe: 4 (over x, core), seq: 2 (over y), mp: 4 (over z).
Axes of the slice: x: 2, y: 2, z: 4, core: 2. Of those that a mesh axis runs over, the one named last changes fastest.
Arguments:
- enc_in: bfloat16 [2, 128, 4096], P(None, 'seq'), may hold values from -6 to 6
- dec_in: bfloat16 [2, 128, 4096], P(None, 'seq'), may hold values from -6 to 6
- doc_ids: int32 [2, 128], replicated, may hold values from 0 to 1, as said below
- enc_sections: int32 [1], replicated, may hold values from 1 to 3
- norm_gain: float32 [4, 4096], P('pipe'), may hold values from 0.1 to 1.9
- q_weight: bfloat16 [4, 4096, 2048], P('pipe', None, 'mp'), may hold values from -0.09375 to 0.09375
- k_weight: bfloat16 [4, 4096, 2048], P('pipe', None, 'mp'), may hold values from -0.09375 to 0.09375
- v_weight: bfloat16 [4, 4096, 2048], P('pipe', None, 'mp'), may hold values from -0.09375 to 0.09375
- o_weight: bfloat16 [4, 2048, 4096], P('pipe', 'mp'), may hold values from -1.25 to 1.25
- out_grad: bfloat16 [2, 128, 4096], P(None, 'seq'), may hold values from -6 to 6
Outputs:
- section_out: bfloat16 [4, 2, 128, 4096], P('pipe', None, 'seq', 'mp')
- section_grad: bfloat16 [4, 2, 2, 128, 4096], P('pipe', None, None, 'seq', 'mp')
The draws below stay inside these ranges and needn't reach their ends.
Inputs may be any that keep to these rules, and one draw needn't show every extreme that they name: `doc_ids`: ids of the two documents that each micro-batch's window holds, shared by its encoder and decoder positions; 0 up to a boundary, 1 after it, each document 64 // 2 or more positions long. Sections with an index below enc_sections[0] are encoder sections, the others decoder sections.
All inputs are finite; a program needn't handle non-finite values.
Results may differ from the reference program's by a relative error of at most 0.034.
Values may be sent and summed in bfloat16 or wider, within the bound.
A program may use at most 192 MiB of HBM per device.

```python
import jax
import jax.numpy as jnp
from jax import lax

D = 4096
HEADS = 8
HS = 256
MB = 2
TOK_DEV = 64
L = 128
N_PIPE = 4


def draw_doc_ids(key, part):
    boundary = jax.random.randint(key, (MB, 1), TOK_DEV // 2, L - TOK_DEV // 2 + 1)
    positions = jnp.arange(L, dtype=jnp.int32)[None, :]
    return (positions >= boundary).astype(jnp.int32)


def shard_levels(key, extent, pieces, low, largest):
    level = 1.0
    for axis_at, blocks in pieces:
        draws = jax.random.uniform(jax.random.fold_in(jax.random.fold_in(key, 6), axis_at), (blocks,), jnp.float32, low / len(pieces), largest / len(pieces))
        level = level * jnp.repeat(jnp.exp(draws), extent[axis_at] // blocks).reshape((-1,) + (1,) * (len(extent) - 1 - axis_at))
    return level


def bell_draw(stream_key, shape, width, bound, pieces=(), kind=jnp.bfloat16):
    result = jax.random.normal(stream_key, shape, jnp.float32) * width
    if len(pieces) > 0:
        result = shard_levels(stream_key, shape, pieces, -0.22, 0.18) * result
    return jnp.clip(result, min=-bound, max=bound).astype(kind)


def setup_inputs(seed: int = 0) -> dict:
    splits = jax.random.split(jax.random.key(seed), 11)
    enc_in = bell_draw(splits[0], (MB, L, D), 1.0, 6.0, ((1, 2),))
    dec_in = bell_draw(splits[1], (MB, L, D), 1.0, 6.0, ((1, 2),))
    doc_ids = draw_doc_ids(jax.random.fold_in(splits[10], 71), 0)
    enc_sections = jax.random.randint(splits[3], (1,), 1, N_PIPE).astype(jnp.int32)
    norm_gain = jnp.clip(1.0 + 0.18 * jax.random.normal(splits[4], (N_PIPE, D), jnp.float32), 0.1, 1.9)
    q_weight = bell_draw(splits[5], (N_PIPE, D, HEADS * HS), D ** -0.5, 0.09375, ((0, 4), (2, 4)))
    k_weight = bell_draw(splits[6], (N_PIPE, D, HEADS * HS), D ** -0.5, 0.09375, ((0, 4), (2, 4)))
    v_weight = bell_draw(splits[7], (N_PIPE, D, HEADS * HS), D ** -0.5, 0.09375, ((0, 4), (2, 4)))
    o_weight = bell_draw(splits[8], (N_PIPE, HEADS * HS, D), (4.0 * (HEADS * HS) ** -0.5), 1.25, ((0, 4), (1, 4)))
    out_grad = bell_draw(splits[9], (MB, L, D), 1.0, 6.0, ((1, 2),))
    return {"enc_in": enc_in, "dec_in": dec_in, "doc_ids": doc_ids, "enc_sections": enc_sections, "norm_gain": norm_gain, "q_weight": q_weight, "k_weight": k_weight, "v_weight": v_weight, "o_weight": o_weight, "out_grad": out_grad}


epsilon = 1e-06

def widened(values):
    return lax.optimization_barrier(values).astype(jnp.float32)

def row_norm(stream, stream_gain):
    values = stream.astype(jnp.float32)
    factor = lax.rsqrt(lax.optimization_barrier(jnp.mean(values * values, axis=-1, keepdims=True)) + epsilon)
    return ((values * factor * stream_gain).astype(jnp.bfloat16), factor)

def head_norm(projected, head_count):
    shaped = projected.reshape(projected.shape[0], head_count, -1)
    factor = lax.rsqrt(lax.optimization_barrier(jnp.mean(shaped * shaped, axis=-1, keepdims=True)) + epsilon)
    return ((shaped * factor).astype(jnp.bfloat16), factor)

def norm_back(stream, factor, stream_gain, incoming):
    values = stream.astype(jnp.float32)
    scaled = stream_gain * incoming
    return factor * (scaled - values * factor * factor * lax.optimization_barrier(jnp.mean(scaled * values, axis=-1, keepdims=True)))

def head_back(normed, factor, incoming):
    values = normed.astype(jnp.float32)
    return factor * (incoming - values * lax.optimization_barrier(jnp.mean(incoming * values, axis=-1, keepdims=True)))

def attend_keys(queries, keys, same_doc):
    scores = jnp.einsum('thd,khd->htk', widened(queries), widened(keys)) * HS ** (-0.5)
    weights = jnp.where(same_doc[None], jnp.exp(scores), jnp.float32(0.0))
    return (weights, lax.optimization_barrier(jnp.sum(weights, axis=-1)))

def section_forward(enc_stream, dec_stream, encoder, stream_gain, query_map, key_map, value_map, out_map, doc_row):
    source = jnp.where(encoder, enc_stream, dec_stream)
    q_in, q_factor = row_norm(source, stream_gain)
    m_in, m_factor = row_norm(enc_stream, stream_gain)
    queries, q_head = head_norm(jnp.dot(q_in, query_map, preferred_element_type=jnp.float32), HEADS)
    keys, k_head = head_norm(jnp.dot(m_in, key_map, preferred_element_type=jnp.float32), HEADS)
    values = jnp.dot(m_in, value_map, preferred_element_type=jnp.float32).astype(jnp.bfloat16)
    values = values.reshape(values.shape[0], HEADS, HS)
    same_doc = doc_row[:, None] == doc_row[None, :]
    weights, totals = attend_keys(queries, keys, same_doc)
    summed = jnp.einsum('htk,khd->thd', widened(weights.astype(jnp.bfloat16)), widened(values))
    attended = (summed / jnp.transpose(totals)[:, :, None]).astype(jnp.bfloat16)
    branch = jnp.dot(attended.reshape(attended.shape[0], -1), out_map, preferred_element_type=jnp.float32)
    updated = (source.astype(jnp.float32) + branch).astype(jnp.bfloat16)
    kept = (source, q_factor, m_factor, queries, q_head, keys, k_head, values, same_doc, attended)
    return (updated, kept)

def section_backward(enc_stream, grad_enc, grad_dec, encoder, stream_gain, query_map, key_map, value_map, out_map, kept):
    source, q_factor, m_factor, queries, q_head, keys, k_head, values, same_doc, attended = kept
    row_count = source.shape[0]
    score_scale = HS ** (-0.5)
    upstream = jnp.where(encoder, grad_enc, grad_dec)
    d_attended = jnp.dot(upstream, out_map.T, preferred_element_type=jnp.float32).astype(jnp.bfloat16)
    d_attended = d_attended.reshape(row_count, HEADS, HS)
    weights, totals = attend_keys(queries, keys, same_doc)
    portion = weights / totals[:, :, None]
    portion_low = portion.astype(jnp.bfloat16)
    along_values = jnp.einsum('thd,khd->htk', widened(d_attended), widened(values))
    delta_rows = lax.optimization_barrier(jnp.sum(widened(d_attended) * widened(attended), axis=-1))
    d_scores = (portion * (along_values - jnp.transpose(delta_rows)[:, :, None])).astype(jnp.bfloat16)
    d_queries = jnp.einsum('htk,khd->thd', widened(d_scores), widened(keys)) * score_scale
    d_keys = jnp.einsum('htk,thd->khd', widened(d_scores), widened(queries)) * score_scale
    d_values = jnp.einsum('htk,thd->khd', widened(portion_low), widened(d_attended)).astype(jnp.bfloat16)
    q_grad = head_back(queries, q_head, d_queries).astype(jnp.bfloat16).reshape(row_count, -1)
    k_grad = head_back(keys, k_head, d_keys).astype(jnp.bfloat16).reshape(row_count, -1)
    d_q_in = jnp.dot(q_grad, query_map.T, preferred_element_type=jnp.float32)
    d_m_in = jnp.dot(k_grad, key_map.T, preferred_element_type=jnp.float32)
    d_m_in = d_m_in + jnp.dot(d_values.reshape(row_count, -1), value_map.T, preferred_element_type=jnp.float32)
    back_q = norm_back(source, q_factor, stream_gain, d_q_in)
    back_m = norm_back(enc_stream, m_factor, stream_gain, d_m_in)
    new_enc = (grad_enc.astype(jnp.float32) + back_m + jnp.where(encoder, back_q, 0.0)).astype(jnp.bfloat16)
    new_dec = (grad_dec.astype(jnp.float32) + jnp.where(encoder, 0.0, back_q)).astype(jnp.bfloat16)
    return (new_enc, new_dec)

def reference(enc_in, dec_in, doc_ids, enc_sections, norm_gain, q_weight, k_weight, v_weight, o_weight, out_grad):
    outs_all = [[None] * MB for section_id in range(N_PIPE)]
    grads_enc = [[None] * MB for section_id in range(N_PIPE)]
    grads_dec = [[None] * MB for section_id in range(N_PIPE)]
    for batch_id in range(MB):
        enc_stream = enc_in[batch_id]
        dec_stream = dec_in[batch_id]
        doc_row = doc_ids[batch_id]
        inputs_kept = []
        for section_id in range(N_PIPE):
            encoder = section_id < enc_sections[0]
            updated, kept = section_forward(enc_stream, dec_stream, encoder, norm_gain[section_id], q_weight[section_id], k_weight[section_id], v_weight[section_id], o_weight[section_id], doc_row)
            inputs_kept.append((enc_stream, kept))
            outs_all[section_id][batch_id] = updated
            enc_stream = jnp.where(encoder, updated, enc_stream)
            dec_stream = jnp.where(encoder, dec_stream, updated)
        grad_enc = jnp.zeros_like(out_grad[batch_id])
        grad_dec = out_grad[batch_id]
        for section_id in range(N_PIPE - 1, -1, -1):
            encoder = section_id < enc_sections[0]
            enc_before, kept = inputs_kept[section_id]
            grad_enc, grad_dec = section_backward(enc_before, grad_enc, grad_dec, encoder, norm_gain[section_id], q_weight[section_id], k_weight[section_id], v_weight[section_id], o_weight[section_id], kept)
            grads_enc[section_id][batch_id] = grad_enc
            grads_dec[section_id][batch_id] = grad_dec
    section_out = jnp.stack([jnp.stack(rows_list) for rows_list in outs_all])
    section_grad = jnp.stack([jnp.stack([jnp.stack(grads_enc[section_id]), jnp.stack(grads_dec[section_id])]) for section_id in range(N_PIPE)])
    return (section_out, section_grad)
```

```python
import functools

import jax
import jax.numpy as jnp
from jax import lax
from jax.experimental import pallas as pl
from jax.experimental.pallas import tpu as pltpu
from jax.sharding import PartitionSpec as P

HEADS = 8
HS = 256
PAD = 128

epsilon = 1e-06
MESH = pl.DeviceIdType.MESH
F32 = jnp.float32
BF16 = jnp.bfloat16


def dot_nn(a, b):
    return jnp.dot(a, b, preferred_element_type=F32)


def dot_nt(a, b):
    return lax.dot_general(a, b, (((1,), (1,)), ((), ())), preferred_element_type=F32)


def dot_tn(a, b):
    return lax.dot_general(a, b, (((0,), (0,)), ((), ())), preferred_element_type=F32)


def kernel(
    n_pipe,
    n_seq,
    n_mp,
    enc_ref,
    dec_ref,
    doc_ref,
    count_ref,
    gain_ref,
    wq_hbm,
    wk_hbm,
    wv_hbm,
    wo_hbm,
    og_ref,
    so_ref,
    sg_ref,
    wq,
    wk,
    wv,
    wo,
    w_sem,
    mask,
    upd_recv,
    enc_recv,
    enc_cur,
    src_cur,
    q_acc,
    k_acc,
    v_acc,
    queries,
    q_factor,
    m_factor,
    q_head,
    k_head,
    kv_all,
    portion,
    attended,
    fs_send,
    fs_recv,
    upd_send,
    u_recv,
    d_att,
    kvg_send,
    kvg_recv,
    q_grad,
    k_grad,
    v_grad,
    dq_buf,
    a_send,
    a_recv,
    b_send,
    b_recv,
    ahop,
    bhop,
    gb_recv,
    upd_ssem,
    upd_rsem,
    enc_ssem,
    enc_rsem,
    kv_ssem,
    kv_rsem,
    fs_ssem,
    fs_rsem,
    u_ssem,
    u_rsem,
    kvg_ssem,
    kvg_rsem,
    a_ssem,
    a_rsem,
    b_ssem,
    b_rsem,
    gb_ssem,
    gb_rsem,
):
    pipe = lax.axis_index("pipe")
    seq = lax.axis_index("seq")
    z = lax.axis_index("mp")
    batches, toks, width = enc_ref.shape
    rows = batches * toks
    share = width // n_mp
    heads = HEADS // n_mp
    units = heads * HS
    scale = HS ** (-0.5)
    last = n_pipe - 1

    def at_mp(j):
        return (pipe, seq, j)

    def at_seq(i):
        return (pipe, i, z)

    def copy(src, dst, ssem, rsem, device):
        return pltpu.make_async_remote_copy(
            src_ref=src,
            dst_ref=dst,
            send_sem=ssem,
            recv_sem=rsem,
            device_id=device,
            device_id_type=MESH,
        )

    weight_loads = [
        pltpu.make_async_copy(hbm.at[0], vmem, w_sem.at[i])
        for i, (hbm, vmem) in enumerate(
            [(wk_hbm, wk), (wv_hbm, wv), (wq_hbm, wq), (wo_hbm, wo)]
        )
    ]
    for load in weight_loads:
        load.start()

    barrier = pltpu.get_barrier_semaphore()
    for k in range(1, n_mp):
        pl.semaphore_signal(
            barrier, inc=1, device_id=at_mp(lax.rem(z + k, n_mp)), device_id_type=MESH
        )
    for k in range(1, n_seq):
        pl.semaphore_signal(
            barrier, inc=1, device_id=at_seq(lax.rem(seq + k, n_seq)), device_id_type=MESH
        )

    @pl.when(pipe > 0)
    def _():
        for j in range(n_mp):
            pl.semaphore_signal(
                barrier, inc=1, device_id=(pipe - 1, seq, j), device_id_type=MESH
            )

    @pl.when(pipe < last)
    def _():
        for j in range(n_mp):
            pl.semaphore_signal(
                barrier, inc=1, device_id=(pipe + 1, seq, j), device_id_type=MESH
            )

    edge = jnp.where(pipe > 0, n_mp, 0) + jnp.where(pipe < last, n_mp, 0)
    pl.semaphore_wait(barrier, n_mp - 1 + n_seq - 1 + edge)

    encoder = pipe < count_ref[0]
    prev_encoder = pipe - 1 < count_ref[0]

    def cut(ref, j):
        lanes = pl.ds(pl.multiple_of(j * share, share), share)
        return ref[:, :, lanes].reshape(rows, share)

    def gain_of(j):
        return gain_ref[:, pl.ds(pl.multiple_of(j * share, share), share)]

    def chunk_rows(ref, j):
        return ref[pl.ds(pl.multiple_of(j * share, share), share), :]

    def chunk_cols(ref, j):
        return ref[:, pl.ds(pl.multiple_of(j * share, share), share)]

    length = n_seq * toks
    for m in range(batches):
        row = doc_ref[m : m + 1, :].astype(F32)
        spread = jnp.broadcast_to(row, (length, length))
        mask[m] = (spread == spread.T).astype(F32)

    @pl.when(pipe == 0)
    def _():
        def fill(j, carry):
            upd_recv[j] = cut(enc_ref, j)
            return carry

        lax.fori_loop(0, n_mp, fill, 0)

    q_acc[...] = jnp.zeros_like(q_acc)
    k_acc[...] = jnp.zeros_like(k_acc)
    v_acc[...] = jnp.zeros_like(v_acc)
    for load in weight_loads[:3]:
        load.wait()

    @pl.when(pipe > 0)
    def _():
        copy(enc_cur, enc_recv, enc_ssem, enc_rsem, at_mp(z)).wait_recv()

    def project(k, sums):
        j = lax.rem(z + k, n_mp)

        @pl.when(pipe > 0)
        def _():
            copy(upd_send, upd_recv.at[j], upd_ssem.at[j], upd_rsem.at[j], at_mp(z)).wait_recv()

        fresh = upd_recv[j].astype(F32)
        enc = jnp.where(prev_encoder, fresh, enc_recv[j].astype(F32))
        dec = jnp.where(prev_encoder, cut(dec_ref, j).astype(F32), fresh)
        src = jnp.where(encoder, enc, dec)
        enc_cur[j] = enc.astype(BF16)
        src_cur[j] = src.astype(BF16)
        gain = gain_of(j)
        m_part = (enc * gain).astype(BF16)
        q_part = (src * gain).astype(BF16)
        k_acc[...] += dot_nn(m_part, chunk_rows(wk, j))
        v_acc[...] += dot_nn(m_part, chunk_rows(wv, j))
        q_acc[...] += dot_nn(q_part, chunk_rows(wq, j))
        return (
            sums[0] + jnp.sum(src * src, axis=-1, keepdims=True),
            sums[1] + jnp.sum(enc * enc, axis=-1, keepdims=True),
        )

    none = jnp.zeros((rows, 1), F32)
    q_square, m_square = lax.fori_loop(0, n_mp, project, (none, none))
    q_factor[...] = lax.rsqrt(q_square / width + epsilon)
    m_factor[...] = lax.rsqrt(m_square / width + epsilon)

    for h in range(heads):
        lanes = slice(h * HS, (h + 1) * HS)
        keys = k_acc[:, lanes] * m_factor[...]
        head = lax.rsqrt(jnp.mean(keys * keys, axis=-1, keepdims=True) + epsilon)
        k_head[h] = head
        kv_all[seq, :, lanes] = (keys * head).astype(BF16)
    kv_all[seq, :, units:] = (v_acc[...] * m_factor[...]).astype(BF16)
    kv_copies = []
    for k in range(1, n_seq):
        peer = lax.rem(seq + k, n_seq)
        moved = copy(
            kv_all.at[seq], kv_all.at[seq], kv_ssem.at[k], kv_rsem.at[seq], at_seq(peer)
        )
        moved.start()
        kv_copies.append(moved)

    @pl.when(pipe < last)
    def _():
        copy(enc_cur, enc_recv, enc_ssem, enc_rsem, (pipe + 1, seq, z)).start()

    for h in range(heads):
        lanes = slice(h * HS, (h + 1) * HS)
        found = q_acc[:, lanes] * q_factor[...]
        head = lax.rsqrt(jnp.mean(found * found, axis=-1, keepdims=True) + epsilon)
        q_head[h] = head
        queries[:, lanes] = (found * head).astype(BF16)

    for k in range(1, n_seq):
        peer = lax.rem(seq + k, n_seq)
        copy(
            kv_all.at[seq], kv_all.at[peer], kv_ssem.at[k], kv_rsem.at[peer], at_seq(peer)
        ).wait_recv()

    def keys_of(m, h):
        lanes = slice(h * HS, (h + 1) * HS)
        return kv_all[:, m * toks : (m + 1) * toks, lanes].reshape(length, HS)

    def values_of(m, h):
        lanes = slice(units + h * HS, units + (h + 1) * HS)
        return kv_all[:, m * toks : (m + 1) * toks, lanes].reshape(length, HS)

    my_rows = pl.ds(pl.multiple_of(seq * toks, toks), toks)
    for m in range(batches):
        span = slice(m * toks, (m + 1) * toks)
        same = mask[m, my_rows, :]
        for h in range(heads):
            lanes = slice(h * HS, (h + 1) * HS)
            scores = dot_nt(queries[span, lanes], keys_of(m, h)) * scale
            weights = jnp.exp(scores) * same
            totals = jnp.sum(weights, axis=-1, keepdims=True)
            summed = dot_nn(weights.astype(BF16), values_of(m, h))
            attended[span, lanes] = (summed / totals).astype(BF16)
            portion[m, h] = weights / totals

    weight_loads[3].wait()

    def emit(k, carry):
        j = lax.rem(z + 1 + k, n_mp)
        fs_send[j] = dot_nn(attended[...], chunk_cols(wo, j)).astype(BF16)

        @pl.when(k < n_mp - 1)
        def _():
            copy(fs_send.at[j], fs_recv.at[z], fs_ssem.at[j], fs_rsem.at[z], at_mp(j)).start()

        return carry

    lax.fori_loop(0, n_mp, emit, 0)
    branch = fs_send[z].astype(F32)
    for k in range(1, n_mp):
        j = lax.rem(z + k, n_mp)
        copy(fs_send.at[j], fs_recv.at[j], fs_ssem.at[j], fs_rsem.at[j], at_mp(j)).wait_recv()
        branch = branch + fs_recv[j].astype(F32)
    updated = (src_cur[z].astype(F32) + branch).astype(BF16)
    upd_send[...] = updated

    @pl.when(pipe < last)
    def _():
        for j in range(n_mp):
            copy(
                upd_send, upd_recv.at[z], upd_ssem.at[j], upd_rsem.at[z], (pipe + 1, seq, j)
            ).start()

    so_ref[0] = updated.reshape(batches, toks, share)

    @pl.when(pipe == last)
    def _():
        def fill(j, carry):
            start = cut(og_ref, j).astype(F32)
            u_recv[j] = jnp.where(encoder, 0.0, start).astype(BF16)
            return carry

        lax.fori_loop(0, n_mp, fill, 0)
        start = cut(og_ref, z).astype(F32)
        gb_recv[...] = jnp.where(encoder, start, 0.0).astype(BF16)

    def pull(k, total):
        j = lax.rem(z + k, n_mp)

        @pl.when(pipe < last)
        def _():
            copy(ahop, u_recv.at[j], u_ssem.at[j], u_rsem.at[j], at_mp(z)).wait_recv()

        return total + dot_nt(u_recv[j], chunk_cols(wo, j))

    d_att[...] = lax.fori_loop(0, n_mp, pull, jnp.zeros((rows, units), F32)).astype(BF16)

    q_stat = none
    for m in range(batches):
        span = slice(m * toks, (m + 1) * toks)
        for h in range(heads):
            lanes = slice(h * HS, (h + 1) * HS)
            wide = slice(units + h * HS, units + (h + 1) * HS)
            keys = keys_of(m, h)
            probs = portion[m, h]
            pulled = d_att[span, lanes]
            along = dot_nt(pulled, values_of(m, h))
            delta = jnp.sum(
                pulled.astype(F32) * attended[span, lanes].astype(F32), axis=-1, keepdims=True
            )
            d_scores = (probs * (along - delta)).astype(BF16)
            asked = queries[span, lanes]
            value_term = dot_tn(probs.astype(BF16), pulled)
            key_term = dot_tn(d_scores, asked) * scale
            kvg_send[:, span, lanes] = key_term.astype(BF16).reshape(n_seq, toks, HS)
            kvg_send[:, span, wide] = value_term.astype(BF16).reshape(n_seq, toks, HS)
            d_queries = dot_nn(d_scores, keys) * scale
            normed = asked.astype(F32)
            mean = jnp.mean(d_queries * normed, axis=-1, keepdims=True)
            q_grad[span, lanes] = (q_head[h, span, :] * (d_queries - normed * mean)).astype(BF16)

    for k in range(1, n_seq):
        peer = lax.rem(seq + k, n_seq)
        copy(
            kvg_send.at[peer], kvg_recv.at[seq], kvg_ssem.at[k], kvg_rsem.at[seq], at_seq(peer)
        ).start()

    q_stat = jnp.sum(q_grad[...].astype(F32) * q_acc[...], axis=-1, keepdims=True)

    def ask(k, carry):
        j = lax.rem(z + 1 + k, n_mp)
        dq_buf[j] = dot_nt(q_grad[...], chunk_rows(wq, j))
        return carry

    lax.fori_loop(0, n_mp, ask, 0)

    d_kv = kvg_send[seq].astype(F32)
    for k in range(1, n_seq):
        peer = lax.rem(seq + k, n_seq)
        copy(
            kvg_send.at[peer], kvg_recv.at[peer], kvg_ssem.at[k], kvg_rsem.at[peer], at_seq(peer)
        ).wait_recv()
        d_kv = d_kv + kvg_recv[peer].astype(F32)
    v_grad[...] = d_kv[:, units:].astype(BF16)
    for h in range(heads):
        lanes = slice(h * HS, (h + 1) * HS)
        d_keys = d_kv[:, lanes]
        normed = kv_all[seq, :, lanes].astype(F32)
        mean = jnp.mean(d_keys * normed, axis=-1, keepdims=True)
        k_grad[:, lanes] = (k_head[h] * (d_keys - normed * mean)).astype(BF16)
    m_stat = jnp.sum(
        k_grad[...].astype(F32) * k_acc[...] + v_grad[...].astype(F32) * v_acc[...],
        axis=-1,
        keepdims=True,
    )

    def sort_a(dq, dm):
        return jnp.where(encoder, dq + dm, jnp.where(prev_encoder, dm, dq))

    def sort_b(dq, dm):
        return jnp.where(encoder, 0.0, jnp.where(prev_encoder, dq, dm))

    a_stat = jnp.broadcast_to(sort_a(q_stat, m_stat), (rows, PAD)).astype(BF16)
    b_stat = jnp.broadcast_to(sort_b(q_stat, m_stat), (rows, PAD)).astype(BF16)

    def spread_out(k, carry):
        j = lax.rem(z + 1 + k, n_mp)
        dm = dot_nt(k_grad[...], chunk_rows(wk, j)) + dot_nt(v_grad[...], chunk_rows(wv, j))
        dq = dq_buf[j]
        a_send[j, :, :share] = sort_a(dq, dm).astype(BF16)
        a_send[j, :, share:] = a_stat

        @pl.when(k < n_mp - 1)
        def _():
            copy(a_send.at[j], a_recv.at[z], a_ssem.at[j], a_rsem.at[z], at_mp(j)).start()

        b_send[j, :, :share] = sort_b(dq, dm).astype(BF16)
        b_send[j, :, share:] = b_stat
        return carry

    lax.fori_loop(0, n_mp, spread_out, 0)

    gain = gain_of(z)
    enc_share = enc_cur[z].astype(F32)
    src_share = src_cur[z].astype(F32)
    own = u_recv[z].astype(F32)

    def norm_back(values, factor, total):
        body = total[:, :share]
        stat = total[:, share : share + 1]
        return factor * (gain * body - values * (factor * factor * (stat / width)))

    total = a_send[z].astype(F32)
    for k in range(1, n_mp):
        j = lax.rem(z + k, n_mp)
        copy(a_send.at[j], a_recv.at[j], a_ssem.at[j], a_rsem.at[j], at_mp(j)).wait_recv()
        total = total + a_recv[j].astype(F32)

    @pl.when(pipe < last)
    def _():
        copy(bhop, gb_recv, gb_ssem, gb_rsem, at_mp(z)).wait_recv()

    other = gb_recv[...].astype(F32)
    turns = jnp.logical_and(jnp.logical_not(encoder), prev_encoder)
    a_values = jnp.where(turns, enc_share, src_share)
    a_factor = jnp.where(turns, m_factor[...], q_factor[...])
    a_new = (jnp.where(turns, other, own) + norm_back(a_values, a_factor, total)).astype(BF16)
    ahop[...] = a_new

    @pl.when(pipe > 0)
    def _():
        for j in range(n_mp):
            copy(ahop, u_recv.at[z], u_ssem.at[j], u_rsem.at[z], (pipe - 1, seq, j)).start()
        for j in range(n_mp):
            copy(ahop, u_recv.at[z], u_ssem.at[j], u_rsem.at[z], (pipe - 1, seq, j)).wait_send()

    for k in range(1, n_mp):
        j = lax.rem(z + k, n_mp)
        copy(b_send.at[j], b_recv.at[z], b_ssem.at[j], b_rsem.at[z], at_mp(j)).start()
    total = b_send[z].astype(F32)
    for k in range(1, n_mp):
        j = lax.rem(z + k, n_mp)
        copy(b_send.at[j], b_recv.at[j], b_ssem.at[j], b_rsem.at[j], at_mp(j)).wait_recv()
        total = total + b_recv[j].astype(F32)
    b_values = jnp.where(turns, src_share, enc_share)
    b_factor = jnp.where(turns, q_factor[...], m_factor[...])
    b_new = (jnp.where(turns, own, other) + norm_back(b_values, b_factor, total)).astype(BF16)
    bhop[...] = b_new

    @pl.when(pipe > 0)
    def _():
        copy(bhop, gb_recv, gb_ssem, gb_rsem, (pipe - 1, seq, z)).start()

    first = jnp.logical_or(encoder, prev_encoder)
    a_wide = a_new.astype(F32)
    b_wide = b_new.astype(F32)
    sg_ref[0, 0] = jnp.where(first, a_wide, b_wide).astype(BF16).reshape(batches, toks, share)
    sg_ref[0, 1] = jnp.where(first, b_wide, a_wide).astype(BF16).reshape(batches, toks, share)

    for moved in kv_copies:
        moved.wait_send()
    for k in range(1, n_seq):
        copy(
            kvg_send.at[seq], kvg_recv.at[seq], kvg_ssem.at[k], kvg_rsem.at[seq], at_seq(seq)
        ).wait_send()
    for k in range(1, n_mp):
        j = lax.rem(z + k, n_mp)
        copy(fs_send.at[j], fs_recv.at[z], fs_ssem.at[j], fs_rsem.at[z], at_mp(j)).wait_send()
        copy(a_send.at[j], a_recv.at[z], a_ssem.at[j], a_rsem.at[z], at_mp(j)).wait_send()
        copy(b_send.at[j], b_recv.at[z], b_ssem.at[j], b_rsem.at[z], at_mp(j)).wait_send()

    @pl.when(pipe < last)
    def _():
        copy(enc_cur, enc_recv, enc_ssem, enc_rsem, (pipe + 1, seq, z)).wait_send()
        for j in range(n_mp):
            copy(
                upd_send, upd_recv.at[z], upd_ssem.at[j], upd_rsem.at[z], (pipe + 1, seq, j)
            ).wait_send()

    @pl.when(pipe > 0)
    def _():
        copy(bhop, gb_recv, gb_ssem, gb_rsem, (pipe - 1, seq, z)).wait_send()


def per_device(n_pipe, n_seq, n_mp, enc_in, dec_in, doc_ids, enc_sections, norm_gain,
               q_weight, k_weight, v_weight, o_weight, out_grad):
    batches, toks, width = enc_in.shape
    rows = batches * toks
    share = width // n_mp
    heads = HEADS // n_mp
    units = heads * HS
    length = n_seq * toks
    vmem = pl.BlockSpec(memory_space=pltpu.VMEM)
    hbm = pl.BlockSpec(memory_space=pl.ANY)
    smem = pl.BlockSpec(memory_space=pltpu.SMEM)
    V = pltpu.VMEM
    dma = pltpu.SemaphoreType.DMA
    scratch = [
        V((width, units), BF16),
        V((width, units), BF16),
        V((width, units), BF16),
        V((units, width), BF16),
        dma((4,)),
        V((batches, length, length), F32),
        V((n_mp, rows, share), BF16),
        V((n_mp, rows, share), BF16),
        V((n_mp, rows, share), BF16),
        V((n_mp, rows, share), BF16),
        V((rows, units), F32),
        V((rows, units), F32),
        V((rows, units), F32),
        V((rows, units), BF16),
        V((rows, 1), F32),
        V((rows, 1), F32),
        V((heads, rows, 1), F32),
        V((heads, rows, 1), F32),
        V((n_seq, rows, 2 * units), BF16),
        V((batches, heads, toks, length), F32),
        V((rows, units), BF16),
        V((n_mp, rows, share), BF16),
        V((n_mp, rows, share), BF16),
        V((rows, share), BF16),
        V((n_mp, rows, share), BF16),
        V((rows, units), BF16),
        V((n_seq, rows, 2 * units), BF16),
        V((n_seq, rows, 2 * units), BF16),
        V((rows, units), BF16),
        V((rows, units), BF16),
        V((rows, units), BF16),
        V((n_mp, rows, share), F32),
        V((n_mp, rows, share + PAD), BF16),
        V((n_mp, rows, share + PAD), BF16),
        V((n_mp, rows, share + PAD), BF16),
        V((n_mp, rows, share + PAD), BF16),
        V((rows, share), BF16),
        V((rows, share), BF16),
        V((rows, share), BF16),
        dma((n_mp,)),
        dma((n_mp,)),
        dma,
        dma,
        dma((n_seq,)),
        dma((n_seq,)),
        dma((n_mp,)),
        dma((n_mp,)),
        dma((n_mp,)),
        dma((n_mp,)),
        dma((n_seq,)),
        dma((n_seq,)),
        dma((n_mp,)),
        dma((n_mp,)),
        dma((n_mp,)),
        dma((n_mp,)),
        dma,
        dma,
    ]
    return pl.pallas_call(
        functools.partial(kernel, n_pipe, n_seq, n_mp),
        out_shape=(
            jax.ShapeDtypeStruct((1, batches, toks, share), BF16),
            jax.ShapeDtypeStruct((1, 2, batches, toks, share), BF16),
        ),
        in_specs=[vmem, vmem, vmem, smem, vmem, hbm, hbm, hbm, hbm, vmem],
        out_specs=(vmem, vmem),
        scratch_shapes=scratch,
        compiler_params=pltpu.CompilerParams(
            collective_id=0, has_side_effects=True, vmem_limit_bytes=56 * 1024 * 1024
        ),
    )(enc_in, dec_in, doc_ids, enc_sections, norm_gain, q_weight, k_weight, v_weight, o_weight,
      out_grad)


def solution(mesh):
    sizes = (mesh.shape["pipe"], mesh.shape["seq"], mesh.shape["mp"])
    return jax.shard_map(
        functools.partial(per_device, *sizes),
        mesh=mesh,
        in_specs=(
            P(None, "seq", None),
            P(None, "seq", None),
            P(),
            P(),
            P("pipe", None),
            P("pipe", None, "mp"),
            P("pipe", None, "mp"),
            P("pipe", None, "mp"),
            P("pipe", "mp", None),
            P(None, "seq", None),
        ),
        out_specs=(P("pipe", None, "seq", "mp"), P("pipe", None, None, "seq", "mp")),
        check_vma=False,
    )
```

```python
import functools

import jax
import jax.numpy as jnp
from jax import lax
from jax.experimental import pallas as pl
from jax.experimental.pallas import tpu as pltpu
from jax.sharding import PartitionSpec as P

HEADS = 8
HS = 256
PAD = 128

epsilon = 1e-06
MESH = pl.DeviceIdType.MESH
F32 = jnp.float32
BF16 = jnp.bfloat16


def dot_nn(a, b):
    return jnp.dot(a, b, preferred_element_type=F32)


def dot_nt(a, b):
    return lax.dot_general(a, b, (((1,), (1,)), ((), ())), preferred_element_type=F32)


def dot_tn(a, b):
    return lax.dot_general(a, b, (((0,), (0,)), ((), ())), preferred_element_type=F32)


def kernel(
    n_pipe,
    n_seq,
    n_mp,
    enc_ref,
    dec_ref,
    doc_ref,
    count_ref,
    gain_ref,
    wq_hbm,
    wk_hbm,
    wv_hbm,
    wo_hbm,
    og_ref,
    so_ref,
    sg_ref,
    wq,
    wk,
    wv,
    wo,
    w_sem,
    mask,
    upd_recv,
    enc_recv,
    enc_cur,
    src_cur,
    q_acc,
    k_acc,
    v_acc,
    queries,
    q_factor,
    m_factor,
    q_head,
    k_head,
    kv_all,
    portion,
    attended,
    fs_send,
    fs_recv,
    upd_send,
    u_recv,
    d_att,
    kvg_send,
    kvg_recv,
    q_grad,
    k_grad,
    v_grad,
    dq_buf,
    a_send,
    a_recv,
    b_send,
    b_recv,
    s_send,
    s_recv,
    s_total,
    ahop,
    bhop,
    gb_recv,
    upd_ssem,
    upd_rsem,
    enc_ssem,
    enc_rsem,
    kv_ssem,
    kv_rsem,
    fs_ssem,
    fs_rsem,
    u_ssem,
    u_rsem,
    kvg_ssem,
    kvg_rsem,
    a_ssem,
    a_rsem,
    b_ssem,
    b_rsem,
    s_ssem,
    s_rsem,
    gb_ssem,
    gb_rsem,
):
    pipe = lax.axis_index("pipe")
    seq = lax.axis_index("seq")
    z = lax.axis_index("mp")
    batches, toks, width = enc_ref.shape
    share = width // n_mp
    heads = HEADS // n_mp
    units = heads * HS
    scale = HS ** (-0.5)
    last = n_pipe - 1

    def at_mp(j):
        return (pipe, seq, j)

    def at_seq(i):
        return (pipe, i, z)

    def copy(src, dst, ssem, rsem, device):
        return pltpu.make_async_remote_copy(
            src_ref=src,
            dst_ref=dst,
            send_sem=ssem,
            recv_sem=rsem,
            device_id=device,
            device_id_type=MESH,
        )

    weight_loads = [
        pltpu.make_async_copy(hbm.at[0], vmem, w_sem.at[i])
        for i, (hbm, vmem) in enumerate(
            [(wk_hbm, wk), (wv_hbm, wv), (wq_hbm, wq), (wo_hbm, wo)]
        )
    ]
    for load in weight_loads:
        load.start()

    barrier = pltpu.get_barrier_semaphore()
    for k in range(1, n_mp):
        pl.semaphore_signal(
            barrier, inc=1, device_id=at_mp(lax.rem(z + k, n_mp)), device_id_type=MESH
        )
    for k in range(1, n_seq):
        pl.semaphore_signal(
            barrier, inc=1, device_id=at_seq(lax.rem(seq + k, n_seq)), device_id_type=MESH
        )

    @pl.when(pipe > 0)
    def _():
        for j in range(n_mp):
            pl.semaphore_signal(
                barrier, inc=1, device_id=(pipe - 1, seq, j), device_id_type=MESH
            )

    @pl.when(pipe < last)
    def _():
        for j in range(n_mp):
            pl.semaphore_signal(
                barrier, inc=1, device_id=(pipe + 1, seq, j), device_id_type=MESH
            )

    edge = jnp.where(pipe > 0, n_mp, 0) + jnp.where(pipe < last, n_mp, 0)
    pl.semaphore_wait(barrier, n_mp - 1 + n_seq - 1 + edge)

    encoder = pipe < count_ref[0]
    prev_encoder = pipe - 1 < count_ref[0]

    def cut(ref, m, j):
        return ref[m, :, pl.ds(pl.multiple_of(j * share, share), share)]

    def gain_of(j):
        return gain_ref[:, pl.ds(pl.multiple_of(j * share, share), share)]

    def chunk_rows(ref, j):
        return ref[pl.ds(pl.multiple_of(j * share, share), share), :]

    def chunk_cols(ref, j):
        return ref[:, pl.ds(pl.multiple_of(j * share, share), share)]

    length = n_seq * toks
    for m in range(batches):
        row = doc_ref[m : m + 1, :].astype(F32)
        spread = jnp.broadcast_to(row, (length, length))
        mask[m] = (spread == spread.T).astype(F32)
    eye = (
        lax.broadcasted_iota(jnp.int32, (toks, PAD), 0)
        == lax.broadcasted_iota(jnp.int32, (toks, PAD), 1)
    ).astype(F32)
    my_rows = pl.ds(pl.multiple_of(seq * toks, toks), toks)
    none = jnp.zeros((toks, 1), F32)

    def keys_of(m, h):
        return kv_all[m, :, :, h * HS : (h + 1) * HS].reshape(length, HS)

    def values_of(m, h):
        return kv_all[m, :, :, units + h * HS : units + (h + 1) * HS].reshape(length, HS)

    def enc_copy(m, device):
        return copy(enc_cur.at[m], enc_recv.at[m], enc_ssem.at[m], enc_rsem.at[m], device)

    def kv_copy(m, slot, peer, owner):
        return copy(
            kv_all.at[m, seq], kv_all.at[m, owner], kv_ssem.at[m, slot], kv_rsem.at[m, owner],
            at_seq(peer),
        )

    def kvg_copy(m, slot, peer, owner):
        return copy(
            kvg_send.at[m, peer], kvg_recv.at[m, owner], kvg_ssem.at[m, slot],
            kvg_rsem.at[m, owner], at_seq(peer),
        )

    def fs_copy(m, j, owner):
        return copy(
            fs_send.at[m, j], fs_recv.at[m, owner], fs_ssem.at[m, j], fs_rsem.at[m, owner],
            at_mp(j),
        )

    def upd_copy(m, j, owner, device):
        return copy(
            upd_send.at[m], upd_recv.at[m, owner], upd_ssem.at[m, j], upd_rsem.at[m, owner],
            device,
        )

    def u_copy(m, j, owner, device):
        return copy(
            ahop.at[m], u_recv.at[m, owner], u_ssem.at[m, j], u_rsem.at[m, owner], device
        )

    def stat_copy(m, j, owner):
        return copy(
            s_send.at[m], s_recv.at[m, owner], s_ssem.at[m, j], s_rsem.at[m, owner], at_mp(j)
        )

    def a_copy(m, j, owner):
        return copy(
            a_send.at[m, j], a_recv.at[m, owner], a_ssem.at[m, j], a_rsem.at[m, owner], at_mp(j)
        )

    def b_copy(m, j, owner):
        return copy(
            b_send.at[m, j], b_recv.at[m, owner], b_ssem.at[m, j], b_rsem.at[m, owner], at_mp(j)
        )

    def gb_copy(m, device):
        return copy(bhop.at[m], gb_recv.at[m], gb_ssem.at[m], gb_rsem.at[m], device)

    def forward_a(m):
        @pl.when(pipe == 0)
        def _():
            def fill(j, carry):
                upd_recv[m, j] = cut(enc_ref, m, j)
                return carry

            lax.fori_loop(0, n_mp, fill, 0)

        @pl.when(pipe > 0)
        def _():
            enc_copy(m, at_mp(z)).wait_recv()

        k_acc[m] = jnp.zeros((toks, units), F32)
        v_acc[m] = jnp.zeros((toks, units), F32)
        q_acc[m] = jnp.zeros((toks, units), F32)

        def project(k, sums):
            j = lax.rem(z + k, n_mp)

            @pl.when(pipe > 0)
            def _():
                upd_copy(m, j, j, at_mp(z)).wait_recv()

            fresh = upd_recv[m, j].astype(F32)
            enc = jnp.where(prev_encoder, fresh, enc_recv[m, j].astype(F32))
            dec = jnp.where(prev_encoder, cut(dec_ref, m, j).astype(F32), fresh)
            src = jnp.where(encoder, enc, dec)
            enc_cur[m, j] = enc.astype(BF16)
            src_cur[m, j] = src.astype(BF16)
            m_part = (enc * gain_of(j)).astype(BF16)
            k_acc[m] += dot_nn(m_part, chunk_rows(wk, j))
            v_acc[m] += dot_nn(m_part, chunk_rows(wv, j))
            return (
                sums[0] + jnp.sum(src * src, axis=-1, keepdims=True),
                sums[1] + jnp.sum(enc * enc, axis=-1, keepdims=True),
            )

        q_square, m_square = lax.fori_loop(0, n_mp, project, (none, none))
        q_factor[m] = lax.rsqrt(q_square / width + epsilon)
        m_factor[m] = lax.rsqrt(m_square / width + epsilon)

        for h in range(heads):
            lanes = slice(h * HS, (h + 1) * HS)
            keys = k_acc[m, :, lanes] * m_factor[m]
            head = lax.rsqrt(jnp.mean(keys * keys, axis=-1, keepdims=True) + epsilon)
            k_head[m, h] = head
            kv_all[m, seq, :, lanes] = (keys * head).astype(BF16)
        kv_all[m, seq, :, units:] = (v_acc[m] * m_factor[m]).astype(BF16)
        for k in range(1, n_seq):
            kv_copy(m, k, lax.rem(seq + k, n_seq), seq).start()

        @pl.when(pipe < last)
        def _():
            enc_copy(m, (pipe + 1, seq, z)).start()

        if m == 0:
            weight_loads[2].wait()

        def project_q(j, carry):
            q_part = (src_cur[m, j].astype(F32) * gain_of(j)).astype(BF16)
            q_acc[m] += dot_nn(q_part, chunk_rows(wq, j))
            return carry

        lax.fori_loop(0, n_mp, project_q, 0)
        for h in range(heads):
            lanes = slice(h * HS, (h + 1) * HS)
            found = q_acc[m, :, lanes] * q_factor[m]
            head = lax.rsqrt(jnp.mean(found * found, axis=-1, keepdims=True) + epsilon)
            q_head[m, h] = head
            queries[m, :, lanes] = (found * head).astype(BF16)

    def forward_b(m):
        for k in range(1, n_seq):
            peer = lax.rem(seq + k, n_seq)
            kv_copy(m, k, peer, peer).wait_recv()
        same = mask[m, my_rows, :]
        for h in range(heads):
            lanes = slice(h * HS, (h + 1) * HS)
            scores = dot_nt(queries[m, :, lanes], keys_of(m, h)) * scale
            weights = jnp.exp(scores) * same
            totals = jnp.sum(weights, axis=-1, keepdims=True)
            summed = dot_nn(weights.astype(BF16), values_of(m, h))
            attended[m, :, lanes] = (summed / totals).astype(BF16)
            portion[m, h] = weights / totals

        if m == 0:
            weight_loads[3].wait()

        def emit(k, carry):
            j = lax.rem(z + 1 + k, n_mp)
            fs_send[m, j] = dot_nn(attended[m], chunk_cols(wo, j)).astype(BF16)

            @pl.when(k < n_mp - 1)
            def _():
                fs_copy(m, j, z).start()

            return carry

        lax.fori_loop(0, n_mp, emit, 0)

    def forward_c(m):
        branch = fs_send[m, z].astype(F32)
        for k in range(1, n_mp):
            j = lax.rem(z + k, n_mp)
            fs_copy(m, j, j).wait_recv()
            branch = branch + fs_recv[m, j].astype(F32)
        updated = (src_cur[m, z].astype(F32) + branch).astype(BF16)
        upd_send[m] = updated

        @pl.when(pipe < last)
        def _():
            for j in range(n_mp):
                upd_copy(m, j, z, (pipe + 1, seq, j)).start()

        so_ref[0, m] = updated

    for load in weight_loads[:2]:
        load.wait()
    forward_a(0)
    forward_b(0)
    for m in range(1, batches):
        forward_a(m)
        forward_c(m - 1)
        forward_b(m)
    forward_c(batches - 1)

    def sort_a(dq, dm):
        return jnp.where(encoder, dq + dm, jnp.where(prev_encoder, dm, dq))

    def sort_b(dq, dm):
        return jnp.where(encoder, 0.0, jnp.where(prev_encoder, dq, dm))

    def to_row(column):
        return jnp.sum(column * eye, axis=0, keepdims=True)

    def to_column(row):
        return jnp.sum(row * eye, axis=1, keepdims=True)

    turns = jnp.logical_and(jnp.logical_not(encoder), prev_encoder)
    first = jnp.logical_or(encoder, prev_encoder)

    def backward_a(m):
        @pl.when(pipe == last)
        def _():
            def fill(j, carry):
                start = cut(og_ref, m, j).astype(F32)
                u_recv[m, j] = jnp.where(encoder, 0.0, start).astype(BF16)
                return carry

            lax.fori_loop(0, n_mp, fill, 0)
            start = cut(og_ref, m, z).astype(F32)
            gb_recv[m] = jnp.where(encoder, start, 0.0).astype(BF16)

        def pull(k, total):
            j = lax.rem(z + k, n_mp)

            @pl.when(pipe < last)
            def _():
                u_copy(m, j, j, at_mp(z)).wait_recv()

            return total + dot_nt(u_recv[m, j], chunk_cols(wo, j))

        d_att[m] = lax.fori_loop(0, n_mp, pull, jnp.zeros((toks, units), F32)).astype(BF16)

        for h in range(heads):
            lanes = slice(h * HS, (h + 1) * HS)
            wide = slice(units + h * HS, units + (h + 1) * HS)
            probs = portion[m, h]
            pulled = d_att[m, :, lanes]
            along = dot_nt(pulled, values_of(m, h))
            delta = jnp.sum(
                pulled.astype(F32) * attended[m, :, lanes].astype(F32), axis=-1, keepdims=True
            )
            d_scores = (probs * (along - delta)).astype(BF16)
            asked = queries[m, :, lanes]
            value_term = dot_tn(probs.astype(BF16), pulled)
            key_term = dot_tn(d_scores, asked) * scale
            kvg_send[m, :, :, lanes] = key_term.astype(BF16).reshape(n_seq, toks, HS)
            kvg_send[m, :, :, wide] = value_term.astype(BF16).reshape(n_seq, toks, HS)
            d_queries = dot_nn(d_scores, keys_of(m, h)) * scale
            normed = asked.astype(F32)
            mean = jnp.mean(d_queries * normed, axis=-1, keepdims=True)
            q_grad[m, :, lanes] = (q_head[m, h] * (d_queries - normed * mean)).astype(BF16)

        for k in range(1, n_seq):
            kvg_copy(m, k, lax.rem(seq + k, n_seq), seq).start()

        def ask(j, carry):
            dq_buf[m, j] = dot_nt(q_grad[m], chunk_rows(wq, j))
            return carry

        lax.fori_loop(0, n_mp, ask, 0)

    def backward_b(m):
        q_stat = jnp.sum(q_grad[m].astype(F32) * q_acc[m], axis=-1, keepdims=True)
        d_kv = kvg_send[m, seq].astype(F32)
        for k in range(1, n_seq):
            peer = lax.rem(seq + k, n_seq)
            kvg_copy(m, k, peer, peer).wait_recv()
            d_kv = d_kv + kvg_recv[m, peer].astype(F32)
        v_grad[m] = d_kv[:, units:].astype(BF16)
        for h in range(heads):
            lanes = slice(h * HS, (h + 1) * HS)
            d_keys = d_kv[:, lanes]
            normed = kv_all[m, seq, :, lanes].astype(F32)
            mean = jnp.mean(d_keys * normed, axis=-1, keepdims=True)
            k_grad[m, :, lanes] = (k_head[m, h] * (d_keys - normed * mean)).astype(BF16)
        m_stat = jnp.sum(
            k_grad[m].astype(F32) * k_acc[m] + v_grad[m].astype(F32) * v_acc[m],
            axis=-1,
            keepdims=True,
        )
        s_send[m, 0:1, :] = to_row(sort_a(q_stat, m_stat))
        s_send[m, 1:2, :] = to_row(sort_b(q_stat, m_stat))
        s_send[m, 2:, :] = jnp.zeros((6, PAD), F32)
        for k in range(1, n_mp):
            stat_copy(m, lax.rem(z + k, n_mp), z).start()

        def spread_out(k, carry):
            j = lax.rem(z + 1 + k, n_mp)
            dm = dot_nt(k_grad[m], chunk_rows(wk, j)) + dot_nt(v_grad[m], chunk_rows(wv, j))
            dq = dq_buf[m, j]
            a_send[m, j] = sort_a(dq, dm).astype(BF16)

            @pl.when(k < n_mp - 1)
            def _():
                a_copy(m, j, z).start()

            b_send[m, j] = sort_b(dq, dm).astype(BF16)
            return carry

        lax.fori_loop(0, n_mp, spread_out, 0)

    def norm_back(values, factor, total, stat):
        return factor * (gain_of(z) * total - values * (factor * factor * (stat / width)))

    def backward_c(m):
        stats = s_send[m]
        for k in range(1, n_mp):
            j = lax.rem(z + k, n_mp)
            stat_copy(m, j, j).wait_recv()
            stats = stats + s_recv[m, j]
        s_total[m] = stats
        total = a_send[m, z].astype(F32)
        for k in range(1, n_mp):
            j = lax.rem(z + k, n_mp)
            a_copy(m, j, j).wait_recv()
            total = total + a_recv[m, j].astype(F32)

        @pl.when(pipe < last)
        def _():
            gb_copy(m, at_mp(z)).wait_recv()

        base = jnp.where(turns, gb_recv[m].astype(F32), u_recv[m, z].astype(F32))
        values = jnp.where(turns, enc_cur[m, z].astype(F32), src_cur[m, z].astype(F32))
        factor = jnp.where(turns, m_factor[m], q_factor[m])
        fresh = base + norm_back(values, factor, total, to_column(stats[0:1, :]))
        ahop[m] = fresh.astype(BF16)

        @pl.when(pipe > 0)
        def _():
            for j in range(n_mp):
                u_copy(m, j, z, (pipe - 1, seq, j)).start()

    def finish(m, b_new):
        a_new = ahop[m].astype(F32)
        sg_ref[0, 0, m] = jnp.where(first, a_new, b_new).astype(BF16)
        sg_ref[0, 1, m] = jnp.where(first, b_new, a_new).astype(BF16)

    def backward_d(m):
        @pl.when(pipe == 0)
        def _():
            finish(m, gb_recv[m].astype(F32))

        @pl.when(pipe > 0)
        def _():
            total = b_send[m, z].astype(F32)
            for k in range(1, n_mp):
                j = lax.rem(z + k, n_mp)
                b_copy(m, j, j).wait_recv()
                total = total + b_recv[m, j].astype(F32)
            base = jnp.where(turns, u_recv[m, z].astype(F32), gb_recv[m].astype(F32))
            values = jnp.where(turns, src_cur[m, z].astype(F32), enc_cur[m, z].astype(F32))
            factor = jnp.where(turns, q_factor[m], m_factor[m])
            fresh = base + norm_back(values, factor, total, to_column(s_total[m, 1:2, :]))
            bhop[m] = fresh.astype(BF16)
            gb_copy(m, (pipe - 1, seq, z)).start()
            finish(m, fresh)

    backward_a(0)
    backward_b(0)
    for m in range(1, batches):
        backward_a(m)
        backward_c(m - 1)
        backward_b(m)
    backward_c(batches - 1)

    @pl.when(pipe > 0)
    def _():
        for m in range(batches):
            for j in range(n_mp):
                u_copy(m, j, z, (pipe - 1, seq, j)).wait_send()
            for k in range(1, n_mp):
                b_copy(m, lax.rem(z + k, n_mp), z).start()

    for m in range(batches):
        backward_d(m)

    for m in range(batches):
        for k in range(1, n_seq):
            peer = lax.rem(seq + k, n_seq)
            kv_copy(m, k, peer, seq).wait_send()
            kvg_copy(m, k, peer, seq).wait_send()
        for k in range(1, n_mp):
            j = lax.rem(z + k, n_mp)
            fs_copy(m, j, z).wait_send()
            stat_copy(m, j, z).wait_send()
            a_copy(m, j, z).wait_send()

    @pl.when(pipe < last)
    def _():
        for m in range(batches):
            enc_copy(m, (pipe + 1, seq, z)).wait_send()
            for j in range(n_mp):
                upd_copy(m, j, z, (pipe + 1, seq, j)).wait_send()

    @pl.when(pipe > 0)
    def _():
        for m in range(batches):
            gb_copy(m, (pipe - 1, seq, z)).wait_send()
            for k in range(1, n_mp):
                b_copy(m, lax.rem(z + k, n_mp), z).wait_send()


def per_device(n_pipe, n_seq, n_mp, enc_in, dec_in, doc_ids, enc_sections, norm_gain,
               q_weight, k_weight, v_weight, o_weight, out_grad):
    batches, toks, width = enc_in.shape
    share = width // n_mp
    heads = HEADS // n_mp
    units = heads * HS
    length = n_seq * toks
    vmem = pl.BlockSpec(memory_space=pltpu.VMEM)
    hbm = pl.BlockSpec(memory_space=pl.ANY)
    smem = pl.BlockSpec(memory_space=pltpu.SMEM)
    V = pltpu.VMEM
    dma = pltpu.SemaphoreType.DMA
    scratch = [
        V((width, units), BF16),
        V((width, units), BF16),
        V((width, units), BF16),
        V((units, width), BF16),
        dma((4,)),
        V((batches, length, length), F32),
        V((batches, n_mp, toks, share), BF16),
        V((batches, n_mp, toks, share), BF16),
        V((batches, n_mp, toks, share), BF16),
        V((batches, n_mp, toks, share), BF16),
        V((batches, toks, units), F32),
        V((batches, toks, units), F32),
        V((batches, toks, units), F32),
        V((batches, toks, units), BF16),
        V((batches, toks, 1), F32),
        V((batches, toks, 1), F32),
        V((batches, heads, toks, 1), F32),
        V((batches, heads, toks, 1), F32),
        V((batches, n_seq, toks, 2 * units), BF16),
        V((batches, heads, toks, length), F32),
        V((batches, toks, units), BF16),
        V((batches, n_mp, toks, share), BF16),
        V((batches, n_mp, toks, share), BF16),
        V((batches, toks, share), BF16),
        V((batches, n_mp, toks, share), BF16),
        V((batches, toks, units), BF16),
        V((batches, n_seq, toks, 2 * units), BF16),
        V((batches, n_seq, toks, 2 * units), BF16),
        V((batches, toks, units), BF16),
        V((batches, toks, units), BF16),
        V((batches, toks, units), BF16),
        V((batches, n_mp, toks, share), F32),
        V((batches, n_mp, toks, share), BF16),
        V((batches, n_mp, toks, share), BF16),
        V((batches, n_mp, toks, share), BF16),
        V((batches, n_mp, toks, share), BF16),
        V((batches, 8, PAD), F32),
        V((batches, n_mp, 8, PAD), F32),
        V((batches, 8, PAD), F32),
        V((batches, toks, share), BF16),
        V((batches, toks, share), BF16),
        V((batches, toks, share), BF16),
        dma((batches, n_mp)),
        dma((batches, n_mp)),
        dma((batches,)),
        dma((batches,)),
        dma((batches, n_seq)),
        dma((batches, n_seq)),
        dma((batches, n_mp)),
        dma((batches, n_mp)),
        dma((batches, n_mp)),
        dma((batches, n_mp)),
        dma((batches, n_seq)),
        dma((batches, n_seq)),
        dma((batches, n_mp)),
        dma((batches, n_mp)),
        dma((batches, n_mp)),
        dma((batches, n_mp)),
        dma((batches, n_mp)),
        dma((batches, n_mp)),
        dma((batches,)),
        dma((batches,)),
    ]
    return pl.pallas_call(
        functools.partial(kernel, n_pipe, n_seq, n_mp),
        out_shape=(
            jax.ShapeDtypeStruct((1, batches, toks, share), BF16),
            jax.ShapeDtypeStruct((1, 2, batches, toks, share), BF16),
        ),
        in_specs=[vmem, vmem, vmem, smem, vmem, hbm, hbm, hbm, hbm, vmem],
        out_specs=(vmem, vmem),
        scratch_shapes=scratch,
        compiler_params=pltpu.CompilerParams(
            collective_id=0, has_side_effects=True, vmem_limit_bytes=56 * 1024 * 1024
        ),
    )(enc_in, dec_in, doc_ids, enc_sections, norm_gain, q_weight, k_weight, v_weight, o_weight,
      out_grad)


def solution(mesh):
    sizes = (mesh.shape["pipe"], mesh.shape["seq"], mesh.shape["mp"])
    return jax.shard_map(
        functools.partial(per_device, *sizes),
        mesh=mesh,
        in_specs=(
            P(None, "seq", None),
            P(None, "seq", None),
            P(),
            P(),
            P("pipe", None),
            P("pipe", None, "mp"),
            P("pipe", None, "mp"),
            P("pipe", None, "mp"),
            P("pipe", "mp", None),
            P(None, "seq", None),
        ),
        out_specs=(P("pipe", None, "seq", "mp"), P("pipe", None, None, "seq", "mp")),
        check_vma=False,
    )
```

```python
import functools

import jax
import jax.numpy as jnp
from jax import lax
from jax.experimental import pallas as pl
from jax.experimental.pallas import tpu as pltpu
from jax.sharding import PartitionSpec as P

HEADS = 8
HS = 256
PAD = 128

epsilon = 1e-06
MESH = pl.DeviceIdType.MESH
F32 = jnp.float32
BF16 = jnp.bfloat16


def dot_nn(a, b):
    return jnp.dot(a, b, preferred_element_type=F32)


def dot_nt(a, b):
    return lax.dot_general(a, b, (((1,), (1,)), ((), ())), preferred_element_type=F32)


def dot_tn(a, b):
    return lax.dot_general(a, b, (((0,), (0,)), ((), ())), preferred_element_type=F32)


def kernel(
    n_pipe,
    n_seq,
    n_mp,
    enc_ref,
    dec_ref,
    doc_ref,
    count_ref,
    gain_ref,
    wq_hbm,
    wk_hbm,
    wv_hbm,
    wo_hbm,
    og_ref,
    so_ref,
    sg_ref,
    wq,
    wk,
    wv,
    wo,
    w_sem,
    mask,
    upd_recv,
    enc_recv,
    enc_cur,
    src_cur,
    q_acc,
    k_acc,
    v_acc,
    queries,
    q_factor,
    m_factor,
    q_head,
    k_head,
    kv_all,
    portion,
    attended,
    fs_send,
    fs_recv,
    upd_send,
    u_recv,
    d_att,
    kvg_send,
    kvg_recv,
    q_grad,
    k_grad,
    v_grad,
    dq_buf,
    a_send,
    a_recv,
    b_send,
    b_recv,
    s_send,
    s_recv,
    s_total,
    fs_relay,
    a_relay,
    b_relay,
    ahop,
    bhop,
    gb_recv,
    upd_ssem,
    upd_rsem,
    enc_ssem,
    enc_rsem,
    kv_ssem,
    kv_rsem,
    fs_ssem,
    fs_rsem,
    u_ssem,
    u_rsem,
    kvg_ssem,
    kvg_rsem,
    a_ssem,
    a_rsem,
    b_ssem,
    b_rsem,
    s_ssem,
    s_rsem,
    relay_ssem,
    relay_rsem,
    pass_ssem,
    gb_ssem,
    gb_rsem,
):
    pipe = lax.axis_index("pipe")
    seq = lax.axis_index("seq")
    z = lax.axis_index("mp")
    batches, toks, width = enc_ref.shape
    share = width // n_mp
    heads = HEADS // n_mp
    units = heads * HS
    scale = HS ** (-0.5)
    last = n_pipe - 1

    def at_mp(j):
        return (pipe, seq, j)

    def at_seq(i):
        return (pipe, i, z)

    def copy(src, dst, ssem, rsem, device):
        return pltpu.make_async_remote_copy(
            src_ref=src,
            dst_ref=dst,
            send_sem=ssem,
            recv_sem=rsem,
            device_id=device,
            device_id_type=MESH,
        )

    weight_loads = [
        pltpu.make_async_copy(hbm.at[0], vmem, w_sem.at[i])
        for i, (hbm, vmem) in enumerate(
            [(wk_hbm, wk), (wv_hbm, wv), (wq_hbm, wq), (wo_hbm, wo)]
        )
    ]
    for load in weight_loads:
        load.start()

    barrier = pltpu.get_barrier_semaphore()
    for k in range(1, n_mp):
        pl.semaphore_signal(
            barrier, inc=1, device_id=at_mp(lax.rem(z + k, n_mp)), device_id_type=MESH
        )
    for k in range(1, n_seq):
        pl.semaphore_signal(
            barrier, inc=1, device_id=at_seq(lax.rem(seq + k, n_seq)), device_id_type=MESH
        )

    @pl.when(pipe > 0)
    def _():
        for j in range(n_mp):
            pl.semaphore_signal(
                barrier, inc=1, device_id=(pipe - 1, seq, j), device_id_type=MESH
            )

    @pl.when(pipe < last)
    def _():
        for j in range(n_mp):
            pl.semaphore_signal(
                barrier, inc=1, device_id=(pipe + 1, seq, j), device_id_type=MESH
            )

    edge = jnp.where(pipe > 0, n_mp, 0) + jnp.where(pipe < last, n_mp, 0)
    pl.semaphore_wait(barrier, n_mp - 1 + n_seq - 1 + edge)

    encoder = pipe < count_ref[0]
    prev_encoder = pipe - 1 < count_ref[0]

    def cut(ref, m, j):
        return ref[m, :, pl.ds(pl.multiple_of(j * share, share), share)]

    def gain_of(j):
        return gain_ref[:, pl.ds(pl.multiple_of(j * share, share), share)]

    def chunk_rows(ref, j):
        return ref[pl.ds(pl.multiple_of(j * share, share), share), :]

    def chunk_cols(ref, j):
        return ref[:, pl.ds(pl.multiple_of(j * share, share), share)]

    length = n_seq * toks
    for m in range(batches):
        row = doc_ref[m : m + 1, :].astype(F32)
        spread = jnp.broadcast_to(row, (length, length))
        mask[m] = (spread == spread.T).astype(F32)
    eye = (
        lax.broadcasted_iota(jnp.int32, (toks, PAD), 0)
        == lax.broadcasted_iota(jnp.int32, (toks, PAD), 1)
    ).astype(F32)
    my_rows = pl.ds(pl.multiple_of(seq * toks, toks), toks)
    none = jnp.zeros((toks, 1), F32)

    def keys_of(m, h):
        return kv_all[m, :, :, h * HS : (h + 1) * HS].reshape(length, HS)

    def values_of(m, h):
        return kv_all[m, :, :, units + h * HS : units + (h + 1) * HS].reshape(length, HS)

    def enc_copy(m, device):
        return copy(enc_cur.at[m], enc_recv.at[m], enc_ssem.at[m], enc_rsem.at[m], device)

    def kv_copy(m, slot, peer, owner):
        return copy(
            kv_all.at[m, seq], kv_all.at[m, owner], kv_ssem.at[m, slot], kv_rsem.at[m, owner],
            at_seq(peer),
        )

    def kvg_copy(m, slot, peer, owner):
        return copy(
            kvg_send.at[m, peer], kvg_recv.at[m, owner], kvg_ssem.at[m, slot],
            kvg_rsem.at[m, owner], at_seq(peer),
        )

    def fs_copy(m, j, owner):
        return copy(
            fs_send.at[m, j], fs_recv.at[m, owner], fs_ssem.at[m, j], fs_rsem.at[m, owner],
            at_mp(j),
        )

    def upd_copy(m, j, owner, device):
        return copy(
            upd_send.at[m], upd_recv.at[m, owner], upd_ssem.at[m, j], upd_rsem.at[m, owner],
            device,
        )

    def u_copy(m, j, owner, device):
        return copy(
            ahop.at[m], u_recv.at[m, owner], u_ssem.at[m, j], u_rsem.at[m, owner], device
        )

    def stat_copy(m, j, owner):
        return copy(
            s_send.at[m], s_recv.at[m, owner], s_ssem.at[m, j], s_rsem.at[m, owner], at_mp(j)
        )

    def a_copy(m, j, owner):
        return copy(
            a_send.at[m, j], a_recv.at[m, owner], a_ssem.at[m, j], a_rsem.at[m, owner], at_mp(j)
        )

    def b_copy(m, j, owner):
        return copy(
            b_send.at[m, j], b_recv.at[m, owner], b_ssem.at[m, j], b_rsem.at[m, owner], at_mp(j)
        )

    def gb_copy(m, device):
        return copy(bhop.at[m], gb_recv.at[m], gb_ssem.at[m], gb_rsem.at[m], device)

    chain = n_mp == 4
    far = n_mp - 1 - z
    upper = z >= n_mp // 2
    near_z = jnp.where(upper, far, z)
    is_end = near_z == 0 if chain else z < 0
    is_mid = near_z == 1 if chain else z < 0
    partner = jnp.where(upper, n_mp - 2, 1)
    other_end = jnp.where(upper, 0, n_mp - 1)
    this_end = jnp.where(upper, n_mp - 1, 0)

    def mirror(j):
        return jnp.where(upper, n_mp - 1 - j, j)

    def reduce_order(k):
        if not chain:
            return lax.rem(z + 1 + k, n_mp)
        mid = jnp.where(k == 0, 2, jnp.where(k == 3, 3, k - 1))
        return mirror(jnp.where(is_end, 3 - k, mid))

    def gather_order(k):
        if not chain:
            return lax.rem(z + k, n_mp)
        mid = jnp.where(k == 0, 1, jnp.where(k == 1, 3, jnp.where(k == 2, 0, 2)))
        return mirror(jnp.where(is_end, k, mid))

    def skipped(j):
        return jnp.logical_and(is_end, j == far)

    def kept(j):
        return jnp.logical_not(skipped(j))

    def relay_copy(which, m, send, relay):
        return copy(
            send.at[m, far], relay.at[m], relay_ssem.at[which, m], relay_rsem.at[which, m],
            at_mp(partner),
        )

    def pass_copy(which, m, buffer, rsem):
        return copy(
            buffer.at[m, other_end], buffer.at[m, other_end], pass_ssem.at[which, m],
            rsem.at[m, other_end], at_mp(this_end),
        )

    def reduce_part(which, m, k, j, block, send, relay, direct):
        send[m, j] = block.astype(BF16)
        closing = jnp.logical_and(is_mid, k == n_mp - 1)
        opening = jnp.logical_and(is_end, k == 0)

        @pl.when(closing)
        def _():
            relay_copy(which, m, send, relay).wait_recv()
            send[m, j] = (block + relay[m].astype(F32)).astype(BF16)

        @pl.when(opening)
        def _():
            relay_copy(which, m, send, relay).start()

        @pl.when(jnp.logical_and(j != z, kept(j)))
        def _():
            direct(m, j, z).start()

    def reduced(m, send, recv, direct):
        total = send[m, z].astype(F32)
        for k in range(1, n_mp):
            j = lax.rem(z + k, n_mp)

            @pl.when(kept(j))
            def _():
                direct(m, j, j).wait_recv()

            total = total + recv[m, j].astype(F32)
        return total

    def reduce_drain(which, m, send, relay, direct):
        for k in range(1, n_mp):
            j = lax.rem(z + k, n_mp)

            @pl.when(kept(j))
            def _():
                direct(m, j, z).wait_send()

        @pl.when(is_end)
        def _():
            relay_copy(which, m, send, relay).wait_send()

    @pl.when(is_end)
    def _():
        for m in range(batches):
            for recv in (fs_recv, a_recv, b_recv):
                recv[m, far] = jnp.zeros((toks, share), BF16)

    hop_order = [lax.rem(z + k, n_mp) for k in sorted(range(n_mp), key=lambda k: (k == 0, k != 2))]

    def forward_a(m):
        @pl.when(pipe == 0)
        def _():
            def fill(j, carry):
                upd_recv[m, j] = cut(enc_ref, m, j)
                return carry

            lax.fori_loop(0, n_mp, fill, 0)

        @pl.when(pipe > 0)
        def _():
            enc_copy(m, at_mp(z)).wait_recv()

        k_acc[m] = jnp.zeros((toks, units), F32)
        v_acc[m] = jnp.zeros((toks, units), F32)
        q_acc[m] = jnp.zeros((toks, units), F32)

        def project(k, sums):
            j = gather_order(k)

            @pl.when(pipe > 0)
            def _():
                upd_copy(m, j, j, at_mp(z)).wait_recv()

                @pl.when(jnp.logical_and(is_mid, k == 1))
                def _():
                    pass_copy(0, m, upd_recv, upd_rsem).start()

            fresh = upd_recv[m, j].astype(F32)
            enc = jnp.where(prev_encoder, fresh, enc_recv[m, j].astype(F32))
            dec = jnp.where(prev_encoder, cut(dec_ref, m, j).astype(F32), fresh)
            src = jnp.where(encoder, enc, dec)
            enc_cur[m, j] = enc.astype(BF16)
            src_cur[m, j] = src.astype(BF16)
            m_part = (enc * gain_of(j)).astype(BF16)
            k_acc[m] += dot_nn(m_part, chunk_rows(wk, j))
            v_acc[m] += dot_nn(m_part, chunk_rows(wv, j))
            return (
                sums[0] + jnp.sum(src * src, axis=-1, keepdims=True),
                sums[1] + jnp.sum(enc * enc, axis=-1, keepdims=True),
            )

        q_square, m_square = lax.fori_loop(0, n_mp, project, (none, none))
        q_factor[m] = lax.rsqrt(q_square / width + epsilon)
        m_factor[m] = lax.rsqrt(m_square / width + epsilon)

        for h in range(heads):
            lanes = slice(h * HS, (h + 1) * HS)
            keys = k_acc[m, :, lanes] * m_factor[m]
            head = lax.rsqrt(jnp.mean(keys * keys, axis=-1, keepdims=True) + epsilon)
            k_head[m, h] = head
            kv_all[m, seq, :, lanes] = (keys * head).astype(BF16)
        kv_all[m, seq, :, units:] = (v_acc[m] * m_factor[m]).astype(BF16)
        for k in range(1, n_seq):
            kv_copy(m, k, lax.rem(seq + k, n_seq), seq).start()

        @pl.when(pipe < last)
        def _():
            enc_copy(m, (pipe + 1, seq, z)).start()

        if m == 0:
            weight_loads[2].wait()

        def project_q(j, carry):
            q_part = (src_cur[m, j].astype(F32) * gain_of(j)).astype(BF16)
            q_acc[m] += dot_nn(q_part, chunk_rows(wq, j))
            return carry

        lax.fori_loop(0, n_mp, project_q, 0)
        for h in range(heads):
            lanes = slice(h * HS, (h + 1) * HS)
            found = q_acc[m, :, lanes] * q_factor[m]
            head = lax.rsqrt(jnp.mean(found * found, axis=-1, keepdims=True) + epsilon)
            q_head[m, h] = head
            queries[m, :, lanes] = (found * head).astype(BF16)

    def forward_b(m):
        for k in range(1, n_seq):
            peer = lax.rem(seq + k, n_seq)
            kv_copy(m, k, peer, peer).wait_recv()
        same = mask[m, my_rows, :]
        for h in range(heads):
            lanes = slice(h * HS, (h + 1) * HS)
            scores = dot_nt(queries[m, :, lanes], keys_of(m, h)) * scale
            weights = jnp.exp(scores) * same
            totals = jnp.sum(weights, axis=-1, keepdims=True)
            summed = dot_nn(weights.astype(BF16), values_of(m, h))
            attended[m, :, lanes] = (summed / totals).astype(BF16)
            portion[m, h] = weights / totals

        if m == 0:
            weight_loads[3].wait()

        def emit(k, carry):
            j = reduce_order(k)
            block = dot_nn(attended[m], chunk_cols(wo, j))
            reduce_part(0, m, k, j, block, fs_send, fs_relay, fs_copy)
            return carry

        lax.fori_loop(0, n_mp, emit, 0)

    def forward_c(m):
        branch = reduced(m, fs_send, fs_recv, fs_copy)
        updated = (src_cur[m, z].astype(F32) + branch).astype(BF16)
        upd_send[m] = updated

        @pl.when(pipe < last)
        def _():
            for j in hop_order:

                @pl.when(kept(j))
                def _():
                    upd_copy(m, j, z, (pipe + 1, seq, j)).start()

        so_ref[0, m] = updated

    for load in weight_loads[:2]:
        load.wait()
    forward_a(0)
    forward_b(0)
    for m in range(1, batches):
        forward_a(m)
        forward_c(m - 1)
        forward_b(m)
    forward_c(batches - 1)

    def sort_a(dq, dm):
        return jnp.where(encoder, dq + dm, jnp.where(prev_encoder, dm, dq))

    def sort_b(dq, dm):
        return jnp.where(encoder, 0.0, jnp.where(prev_encoder, dq, dm))

    def to_row(column):
        return jnp.sum(column * eye, axis=0, keepdims=True)

    def to_column(row):
        return jnp.sum(row * eye, axis=1, keepdims=True)

    turns = jnp.logical_and(jnp.logical_not(encoder), prev_encoder)
    first = jnp.logical_or(encoder, prev_encoder)

    def backward_a(m):
        @pl.when(pipe == last)
        def _():
            def fill(j, carry):
                start = cut(og_ref, m, j).astype(F32)
                u_recv[m, j] = jnp.where(encoder, 0.0, start).astype(BF16)
                return carry

            lax.fori_loop(0, n_mp, fill, 0)
            start = cut(og_ref, m, z).astype(F32)
            gb_recv[m] = jnp.where(encoder, start, 0.0).astype(BF16)

        def pull(k, total):
            j = gather_order(k)

            @pl.when(pipe < last)
            def _():
                u_copy(m, j, j, at_mp(z)).wait_recv()

                @pl.when(jnp.logical_and(is_mid, k == 1))
                def _():
                    pass_copy(1, m, u_recv, u_rsem).start()

            return total + dot_nt(u_recv[m, j], chunk_cols(wo, j))

        d_att[m] = lax.fori_loop(0, n_mp, pull, jnp.zeros((toks, units), F32)).astype(BF16)

        for h in range(heads):
            lanes = slice(h * HS, (h + 1) * HS)
            wide = slice(units + h * HS, units + (h + 1) * HS)
            probs = portion[m, h]
            pulled = d_att[m, :, lanes]
            along = dot_nt(pulled, values_of(m, h))
            delta = jnp.sum(
                pulled.astype(F32) * attended[m, :, lanes].astype(F32), axis=-1, keepdims=True
            )
            d_scores = (probs * (along - delta)).astype(BF16)
            asked = queries[m, :, lanes]
            value_term = dot_tn(probs.astype(BF16), pulled)
            key_term = dot_tn(d_scores, asked) * scale
            kvg_send[m, :, :, lanes] = key_term.astype(BF16).reshape(n_seq, toks, HS)
            kvg_send[m, :, :, wide] = value_term.astype(BF16).reshape(n_seq, toks, HS)
            d_queries = dot_nn(d_scores, keys_of(m, h)) * scale
            normed = asked.astype(F32)
            mean = jnp.mean(d_queries * normed, axis=-1, keepdims=True)
            q_grad[m, :, lanes] = (q_head[m, h] * (d_queries - normed * mean)).astype(BF16)

        for k in range(1, n_seq):
            kvg_copy(m, k, lax.rem(seq + k, n_seq), seq).start()

        def ask(j, carry):
            dq_buf[m, j] = dot_nt(q_grad[m], chunk_rows(wq, j))
            return carry

        lax.fori_loop(0, n_mp, ask, 0)

    def backward_b(m):
        q_stat = jnp.sum(q_grad[m].astype(F32) * q_acc[m], axis=-1, keepdims=True)
        d_kv = kvg_send[m, seq].astype(F32)
        for k in range(1, n_seq):
            peer = lax.rem(seq + k, n_seq)
            kvg_copy(m, k, peer, peer).wait_recv()
            d_kv = d_kv + kvg_recv[m, peer].astype(F32)
        v_grad[m] = d_kv[:, units:].astype(BF16)
        for h in range(heads):
            lanes = slice(h * HS, (h + 1) * HS)
            d_keys = d_kv[:, lanes]
            normed = kv_all[m, seq, :, lanes].astype(F32)
            mean = jnp.mean(d_keys * normed, axis=-1, keepdims=True)
            k_grad[m, :, lanes] = (k_head[m, h] * (d_keys - normed * mean)).astype(BF16)
        m_stat = jnp.sum(
            k_grad[m].astype(F32) * k_acc[m] + v_grad[m].astype(F32) * v_acc[m],
            axis=-1,
            keepdims=True,
        )
        s_send[m, 0:1, :] = to_row(sort_a(q_stat, m_stat))
        s_send[m, 1:2, :] = to_row(sort_b(q_stat, m_stat))
        s_send[m, 2:, :] = jnp.zeros((6, PAD), F32)
        for k in range(1, n_mp):
            stat_copy(m, lax.rem(z + k, n_mp), z).start()

        def spread_out(k, carry):
            j = reduce_order(k)
            dm = dot_nt(k_grad[m], chunk_rows(wk, j)) + dot_nt(v_grad[m], chunk_rows(wv, j))
            dq = dq_buf[m, j]
            reduce_part(1, m, k, j, sort_a(dq, dm), a_send, a_relay, a_copy)
            b_send[m, j] = sort_b(dq, dm).astype(BF16)
            return carry

        lax.fori_loop(0, n_mp, spread_out, 0)

    def norm_back(values, factor, total, stat):
        return factor * (gain_of(z) * total - values * (factor * factor * (stat / width)))

    def backward_c(m):
        stats = s_send[m]
        for k in range(1, n_mp):
            j = lax.rem(z + k, n_mp)
            stat_copy(m, j, j).wait_recv()
            stats = stats + s_recv[m, j]
        s_total[m] = stats
        total = reduced(m, a_send, a_recv, a_copy)

        @pl.when(pipe < last)
        def _():
            gb_copy(m, at_mp(z)).wait_recv()

        base = jnp.where(turns, gb_recv[m].astype(F32), u_recv[m, z].astype(F32))
        values = jnp.where(turns, enc_cur[m, z].astype(F32), src_cur[m, z].astype(F32))
        factor = jnp.where(turns, m_factor[m], q_factor[m])
        fresh = base + norm_back(values, factor, total, to_column(stats[0:1, :]))
        ahop[m] = fresh.astype(BF16)

        @pl.when(pipe > 0)
        def _():
            for j in hop_order:

                @pl.when(kept(j))
                def _():
                    u_copy(m, j, z, (pipe - 1, seq, j)).start()

    def finish(m, b_new):
        a_new = ahop[m].astype(F32)
        sg_ref[0, 0, m] = jnp.where(first, a_new, b_new).astype(BF16)
        sg_ref[0, 1, m] = jnp.where(first, b_new, a_new).astype(BF16)

    def backward_d(m):
        @pl.when(pipe == 0)
        def _():
            finish(m, gb_recv[m].astype(F32))

        @pl.when(pipe > 0)
        def _():
            total = reduced(m, b_send, b_recv, b_copy)
            base = jnp.where(turns, u_recv[m, z].astype(F32), gb_recv[m].astype(F32))
            values = jnp.where(turns, src_cur[m, z].astype(F32), enc_cur[m, z].astype(F32))
            factor = jnp.where(turns, q_factor[m], m_factor[m])
            fresh = base + norm_back(values, factor, total, to_column(s_total[m, 1:2, :]))
            bhop[m] = fresh.astype(BF16)
            gb_copy(m, (pipe - 1, seq, z)).start()
            finish(m, fresh)

    backward_a(0)
    backward_b(0)
    for m in range(1, batches):
        backward_a(m)
        backward_c(m - 1)
        backward_b(m)
    backward_c(batches - 1)

    @pl.when(pipe > 0)
    def _():
        for m in range(batches):
            for j in hop_order:

                @pl.when(kept(j))
                def _():
                    u_copy(m, j, z, (pipe - 1, seq, j)).wait_send()

            @pl.when(is_end)
            def _():
                relay_copy(2, m, b_send, b_relay).start()

            for k in range(1, n_mp):
                j = lax.rem(z + k, n_mp)
                held = jnp.logical_and(is_mid, j == other_end)

                @pl.when(jnp.logical_and(kept(j), jnp.logical_not(held)))
                def _():
                    b_copy(m, j, z).start()

        @pl.when(is_mid)
        def _():
            for m in range(batches):
                relay_copy(2, m, b_send, b_relay).wait_recv()
                joined = b_send[m, other_end].astype(F32) + b_relay[m].astype(F32)
                b_send[m, other_end] = joined.astype(BF16)
                b_copy(m, other_end, z).start()

    for m in range(batches):
        backward_d(m)

    for m in range(batches):
        for k in range(1, n_seq):
            peer = lax.rem(seq + k, n_seq)
            kv_copy(m, k, peer, seq).wait_send()
            kvg_copy(m, k, peer, seq).wait_send()
        for k in range(1, n_mp):
            j = lax.rem(z + k, n_mp)
            stat_copy(m, j, z).wait_send()
        reduce_drain(0, m, fs_send, fs_relay, fs_copy)
        reduce_drain(1, m, a_send, a_relay, a_copy)

    @pl.when(pipe < last)
    def _():
        for m in range(batches):
            enc_copy(m, (pipe + 1, seq, z)).wait_send()
            for j in hop_order:

                @pl.when(kept(j))
                def _():
                    upd_copy(m, j, z, (pipe + 1, seq, j)).wait_send()

            @pl.when(is_mid)
            def _():
                pass_copy(1, m, u_recv, u_rsem).wait_send()

    @pl.when(pipe > 0)
    def _():
        for m in range(batches):
            gb_copy(m, (pipe - 1, seq, z)).wait_send()
            reduce_drain(2, m, b_send, b_relay, b_copy)

            @pl.when(is_mid)
            def _():
                pass_copy(0, m, upd_recv, upd_rsem).wait_send()


def per_device(n_pipe, n_seq, n_mp, enc_in, dec_in, doc_ids, enc_sections, norm_gain,
               q_weight, k_weight, v_weight, o_weight, out_grad):
    batches, toks, width = enc_in.shape
    share = width // n_mp
    heads = HEADS // n_mp
    units = heads * HS
    length = n_seq * toks
    vmem = pl.BlockSpec(memory_space=pltpu.VMEM)
    hbm = pl.BlockSpec(memory_space=pl.ANY)
    smem = pl.BlockSpec(memory_space=pltpu.SMEM)
    V = pltpu.VMEM
    dma = pltpu.SemaphoreType.DMA
    scratch = [
        V((width, units), BF16),
        V((width, units), BF16),
        V((width, units), BF16),
        V((units, width), BF16),
        dma((4,)),
        V((batches, length, length), F32),
        V((batches, n_mp, toks, share), BF16),
        V((batches, n_mp, toks, share), BF16),
        V((batches, n_mp, toks, share), BF16),
        V((batches, n_mp, toks, share), BF16),
        V((batches, toks, units), F32),
        V((batches, toks, units), F32),
        V((batches, toks, units), F32),
        V((batches, toks, units), BF16),
        V((batches, toks, 1), F32),
        V((batches, toks, 1), F32),
        V((batches, heads, toks, 1), F32),
        V((batches, heads, toks, 1), F32),
        V((batches, n_seq, toks, 2 * units), BF16),
        V((batches, heads, toks, length), F32),
        V((batches, toks, units), BF16),
        V((batches, n_mp, toks, share), BF16),
        V((batches, n_mp, toks, share), BF16),
        V((batches, toks, share), BF16),
        V((batches, n_mp, toks, share), BF16),
        V((batches, toks, units), BF16),
        V((batches, n_seq, toks, 2 * units), BF16),
        V((batches, n_seq, toks, 2 * units), BF16),
        V((batches, toks, units), BF16),
        V((batches, toks, units), BF16),
        V((batches, toks, units), BF16),
        V((batches, n_mp, toks, share), F32),
        V((batches, n_mp, toks, share), BF16),
        V((batches, n_mp, toks, share), BF16),
        V((batches, n_mp, toks, share), BF16),
        V((batches, n_mp, toks, share), BF16),
        V((batches, 8, PAD), F32),
        V((batches, n_mp, 8, PAD), F32),
        V((batches, 8, PAD), F32),
        V((batches, toks, share), BF16),
        V((batches, toks, share), BF16),
        V((batches, toks, share), BF16),
        V((batches, toks, share), BF16),
        V((batches, toks, share), BF16),
        V((batches, toks, share), BF16),
        dma((batches, n_mp)),
        dma((batches, n_mp)),
        dma((batches,)),
        dma((batches,)),
        dma((batches, n_seq)),
        dma((batches, n_seq)),
        dma((batches, n_mp)),
        dma((batches, n_mp)),
        dma((batches, n_mp)),
        dma((batches, n_mp)),
        dma((batches, n_seq)),
        dma((batches, n_seq)),
        dma((batches, n_mp)),
        dma((batches, n_mp)),
        dma((batches, n_mp)),
        dma((batches, n_mp)),
        dma((batches, n_mp)),
        dma((batches, n_mp)),
        dma((3, batches)),
        dma((3, batches)),
        dma((2, batches)),
        dma((batches,)),
        dma((batches,)),
    ]
    return pl.pallas_call(
        functools.partial(kernel, n_pipe, n_seq, n_mp),
        out_shape=(
            jax.ShapeDtypeStruct((1, batches, toks, share), BF16),
            jax.ShapeDtypeStruct((1, 2, batches, toks, share), BF16),
        ),
        in_specs=[vmem, vmem, vmem, smem, vmem, hbm, hbm, hbm, hbm, vmem],
        out_specs=(vmem, vmem),
        scratch_shapes=scratch,
        compiler_params=pltpu.CompilerParams(
            collective_id=0, has_side_effects=True, vmem_limit_bytes=56 * 1024 * 1024
        ),
    )(enc_in, dec_in, doc_ids, enc_sections, norm_gain, q_weight, k_weight, v_weight, o_weight,
      out_grad)


def solution(mesh):
    sizes = (mesh.shape["pipe"], mesh.shape["seq"], mesh.shape["mp"])
    return jax.shard_map(
        functools.partial(per_device, *sizes),
        mesh=mesh,
        in_specs=(
            P(None, "seq", None),
            P(None, "seq", None),
            P(),
            P(),
            P("pipe", None),
            P("pipe", None, "mp"),
            P("pipe", None, "mp"),
            P("pipe", None, "mp"),
            P("pipe", "mp", None),
            P(None, "seq", None),
        ),
        out_specs=(P("pipe", None, "seq", "mp"), P("pipe", None, None, "seq", "mp")),
        check_vma=False,
    )
```

```python
import functools

import jax
import jax.numpy as jnp
from jax import lax
from jax.experimental import pallas as pl
from jax.experimental.pallas import tpu as pltpu
from jax.sharding import PartitionSpec as P

HEADS = 8
HS = 256
PAD = 128

epsilon = 1e-06
MESH = pl.DeviceIdType.MESH
F32 = jnp.float32
BF16 = jnp.bfloat16


def dot_nn(a, b):
    return jnp.dot(a, b, preferred_element_type=F32)


def dot_nt(a, b):
    return lax.dot_general(a, b, (((1,), (1,)), ((), ())), preferred_element_type=F32)


def dot_tn(a, b):
    return lax.dot_general(a, b, (((0,), (0,)), ((), ())), preferred_element_type=F32)


def kernel(
    n_pipe,
    n_seq,
    n_mp,
    enc_ref,
    dec_ref,
    doc_ref,
    count_ref,
    gain_ref,
    wq_hbm,
    wk_hbm,
    wv_hbm,
    wo_hbm,
    og_ref,
    so_ref,
    sg_ref,
    wq,
    wk,
    wv,
    wo,
    w_sem,
    mask,
    upd_recv,
    enc_recv,
    enc_cur,
    src_cur,
    q_acc,
    k_acc,
    v_acc,
    queries,
    q_factor,
    m_factor,
    q_head,
    k_head,
    kv_all,
    portion,
    attended,
    fs_send,
    fs_recv,
    upd_send,
    u_recv,
    d_att,
    kvg_send,
    kvg_recv,
    q_grad,
    k_grad,
    v_grad,
    dq_buf,
    a_send,
    a_recv,
    b_send,
    b_recv,
    s_send,
    s_recv,
    s_total,
    fs_relay,
    a_relay,
    b_relay,
    ahop,
    bhop,
    gb_recv,
    upd_ssem,
    upd_rsem,
    enc_ssem,
    enc_rsem,
    kv_ssem,
    kv_rsem,
    fs_ssem,
    fs_rsem,
    u_ssem,
    u_rsem,
    kvg_ssem,
    kvg_rsem,
    a_ssem,
    a_rsem,
    b_ssem,
    b_rsem,
    s_ssem,
    s_rsem,
    relay_ssem,
    relay_rsem,
    pass_ssem,
    gb_ssem,
    gb_rsem,
):
    pipe = lax.axis_index("pipe")
    seq = lax.axis_index("seq")
    z = lax.axis_index("mp")
    batches, toks, width = enc_ref.shape
    share = width // n_mp
    heads = HEADS // n_mp
    units = heads * HS
    scale = HS ** (-0.5)
    last = n_pipe - 1

    def at_mp(j):
        return (pipe, seq, j)

    def at_seq(i):
        return (pipe, i, z)

    def copy(src, dst, ssem, rsem, device):
        return pltpu.make_async_remote_copy(
            src_ref=src,
            dst_ref=dst,
            send_sem=ssem,
            recv_sem=rsem,
            device_id=device,
            device_id_type=MESH,
        )

    weight_loads = [
        pltpu.make_async_copy(hbm.at[0], vmem, w_sem.at[i])
        for i, (hbm, vmem) in enumerate(
            [(wk_hbm, wk), (wv_hbm, wv), (wq_hbm, wq), (wo_hbm, wo)]
        )
    ]
    for load in weight_loads:
        load.start()

    barrier = pltpu.get_barrier_semaphore()
    for k in range(1, n_mp):
        pl.semaphore_signal(
            barrier, inc=1, device_id=at_mp(lax.rem(z + k, n_mp)), device_id_type=MESH
        )
    for k in range(1, n_seq):
        pl.semaphore_signal(
            barrier, inc=1, device_id=at_seq(lax.rem(seq + k, n_seq)), device_id_type=MESH
        )

    @pl.when(pipe > 0)
    def _():
        for j in range(n_mp):
            pl.semaphore_signal(
                barrier, inc=1, device_id=(pipe - 1, seq, j), device_id_type=MESH
            )

    @pl.when(pipe < last)
    def _():
        for j in range(n_mp):
            pl.semaphore_signal(
                barrier, inc=1, device_id=(pipe + 1, seq, j), device_id_type=MESH
            )

    edge = jnp.where(pipe > 0, n_mp, 0) + jnp.where(pipe < last, n_mp, 0)
    pl.semaphore_wait(barrier, n_mp - 1 + n_seq - 1 + edge)

    encoder = pipe < count_ref[0]
    prev_encoder = pipe - 1 < count_ref[0]

    def cut(ref, m, j):
        return ref[m, :, pl.ds(pl.multiple_of(j * share, share), share)]

    def gain_of(j):
        return gain_ref[:, pl.ds(pl.multiple_of(j * share, share), share)]

    def chunk_rows(ref, j):
        return ref[pl.ds(pl.multiple_of(j * share, share), share), :]

    def chunk_cols(ref, j):
        return ref[:, pl.ds(pl.multiple_of(j * share, share), share)]

    length = n_seq * toks
    for m in range(batches):
        row = doc_ref[m : m + 1, :].astype(F32)
        spread = jnp.broadcast_to(row, (length, length))
        mask[m] = (spread == spread.T).astype(F32)
    eye = (
        lax.broadcasted_iota(jnp.int32, (toks, PAD), 0)
        == lax.broadcasted_iota(jnp.int32, (toks, PAD), 1)
    ).astype(F32)
    my_rows = pl.ds(pl.multiple_of(seq * toks, toks), toks)
    none = jnp.zeros((toks, 1), F32)

    def keys_of(m, h):
        return kv_all[m, :, :, h * HS : (h + 1) * HS].reshape(length, HS)

    def values_of(m, h):
        return kv_all[m, :, :, units + h * HS : units + (h + 1) * HS].reshape(length, HS)

    def enc_copy(m, device):
        return copy(enc_cur.at[m], enc_recv.at[m], enc_ssem.at[m], enc_rsem.at[m], device)

    def kv_copy(m, slot, peer, owner):
        return copy(
            kv_all.at[m, seq], kv_all.at[m, owner], kv_ssem.at[m, slot], kv_rsem.at[m, owner],
            at_seq(peer),
        )

    def kvg_copy(m, slot, peer, owner):
        return copy(
            kvg_send.at[m, peer], kvg_recv.at[m, owner], kvg_ssem.at[m, slot],
            kvg_rsem.at[m, owner], at_seq(peer),
        )

    def fs_copy(m, j, owner):
        return copy(
            fs_send.at[m, j], fs_recv.at[m, owner], fs_ssem.at[m, j], fs_rsem.at[m, owner],
            at_mp(j),
        )

    def upd_copy(m, j, owner, device):
        return copy(
            upd_send.at[m], upd_recv.at[m, owner], upd_ssem.at[m, j], upd_rsem.at[m, owner],
            device,
        )

    def u_copy(m, j, owner, device):
        return copy(
            ahop.at[m], u_recv.at[m, owner], u_ssem.at[m, j], u_rsem.at[m, owner], device
        )

    def stat_copy(m, j, owner):
        return copy(
            s_send.at[m], s_recv.at[m, owner], s_ssem.at[m, j], s_rsem.at[m, owner], at_mp(j)
        )

    def a_copy(m, j, owner):
        return copy(
            a_send.at[m, j], a_recv.at[m, owner], a_ssem.at[m, j], a_rsem.at[m, owner], at_mp(j)
        )

    def b_copy(m, j, owner):
        return copy(
            b_send.at[m, j], b_recv.at[m, owner], b_ssem.at[m, j], b_rsem.at[m, owner], at_mp(j)
        )

    def gb_copy(m, device):
        return copy(bhop.at[m], gb_recv.at[m], gb_ssem.at[m], gb_rsem.at[m], device)

    chain = n_mp == 4
    far = n_mp - 1 - z
    upper = z >= n_mp // 2
    near_z = jnp.where(upper, far, z)
    is_end = near_z == 0 if chain else z < 0
    is_mid = near_z == 1 if chain else z < 0
    partner = jnp.where(upper, n_mp - 2, 1)
    other_end = jnp.where(upper, 0, n_mp - 1)
    this_end = jnp.where(upper, n_mp - 1, 0)

    def mirror(j):
        return jnp.where(upper, n_mp - 1 - j, j)

    def reduce_order(k):
        if not chain:
            return lax.rem(z + 1 + k, n_mp)
        mid = jnp.where(k == 0, 2, jnp.where(k == 3, 3, k - 1))
        return mirror(jnp.where(is_end, 3 - k, mid))

    def gather_order(k):
        if not chain:
            return lax.rem(z + k, n_mp)
        mid = jnp.where(k == 0, 1, jnp.where(k == 1, 3, jnp.where(k == 2, 0, 2)))
        return mirror(jnp.where(is_end, k, mid))

    def skipped(j):
        return jnp.logical_and(is_end, j == far)

    def kept(j):
        return jnp.logical_not(skipped(j))

    def relay_copy(which, m, send, relay):
        return copy(
            send.at[m, far], relay.at[m], relay_ssem.at[which, m], relay_rsem.at[which, m],
            at_mp(partner),
        )

    def pass_copy(which, m, buffer, rsem):
        return copy(
            buffer.at[m, other_end], buffer.at[m, other_end], pass_ssem.at[which, m],
            rsem.at[m, other_end], at_mp(this_end),
        )

    def reduce_part(which, m, k, j, block, send, relay, direct):
        send[m, j] = block.astype(BF16)
        closing = jnp.logical_and(is_mid, k == n_mp - 1)
        opening = jnp.logical_and(is_end, k == 0)

        @pl.when(closing)
        def _():
            relay_copy(which, m, send, relay).wait_recv()
            send[m, j] = (block + relay[m].astype(F32)).astype(BF16)

        @pl.when(opening)
        def _():
            relay_copy(which, m, send, relay).start()

        @pl.when(jnp.logical_and(j != z, kept(j)))
        def _():
            direct(m, j, z).start()

    def reduced(m, send, recv, direct):
        total = send[m, z].astype(F32)
        for k in range(1, n_mp):
            j = lax.rem(z + k, n_mp)

            @pl.when(kept(j))
            def _():
                direct(m, j, j).wait_recv()

            total = total + recv[m, j].astype(F32)
        return total

    def reduce_drain(which, m, send, relay, direct):
        for k in range(1, n_mp):
            j = lax.rem(z + k, n_mp)

            @pl.when(kept(j))
            def _():
                direct(m, j, z).wait_send()

        @pl.when(is_end)
        def _():
            relay_copy(which, m, send, relay).wait_send()

    @pl.when(is_end)
    def _():
        for m in range(batches):
            for recv in (fs_recv, a_recv, b_recv):
                recv[m, far] = jnp.zeros((toks, share), BF16)

    hop_order = [lax.rem(z + k, n_mp) for k in sorted(range(n_mp), key=lambda k: (k == 0, k != 2))]

    def forward_a(m, wait_q):
        @pl.when(pipe == 0)
        def _():
            def fill(j, carry):
                upd_recv[m, j] = cut(enc_ref, m, j)
                return carry

            lax.fori_loop(0, n_mp, fill, 0)

        @pl.when(pipe > 1)
        def _():
            enc_copy(m, at_mp(z)).wait_recv()

        k_acc[m] = jnp.zeros((toks, units), F32)
        v_acc[m] = jnp.zeros((toks, units), F32)
        q_acc[m] = jnp.zeros((toks, units), F32)

        def project(k, sums):
            j = gather_order(k)

            @pl.when(pipe > 0)
            def _():
                upd_copy(m, j, j, at_mp(z)).wait_recv()

                @pl.when(jnp.logical_and(is_mid, k == 1))
                def _():
                    pass_copy(0, m, upd_recv, upd_rsem).start()

            fresh = upd_recv[m, j].astype(F32)
            enc = jnp.where(prev_encoder, fresh, enc_recv[m, j].astype(F32))
            dec = jnp.where(prev_encoder, cut(dec_ref, m, j).astype(F32), fresh)
            src = jnp.where(encoder, enc, dec)
            enc_cur[m, j] = enc.astype(BF16)
            src_cur[m, j] = src.astype(BF16)
            m_part = (enc * gain_of(j)).astype(BF16)
            k_acc[m] += dot_nn(m_part, chunk_rows(wk, j))
            v_acc[m] += dot_nn(m_part, chunk_rows(wv, j))
            return (
                sums[0] + jnp.sum(src * src, axis=-1, keepdims=True),
                sums[1] + jnp.sum(enc * enc, axis=-1, keepdims=True),
            )

        q_square, m_square = lax.fori_loop(0, n_mp, project, (none, none))
        q_factor[m] = lax.rsqrt(q_square / width + epsilon)
        m_factor[m] = lax.rsqrt(m_square / width + epsilon)

        for h in range(heads):
            lanes = slice(h * HS, (h + 1) * HS)
            keys = k_acc[m, :, lanes] * m_factor[m]
            head = lax.rsqrt(jnp.mean(keys * keys, axis=-1, keepdims=True) + epsilon)
            k_head[m, h] = head
            kv_all[m, seq, :, lanes] = (keys * head).astype(BF16)
        kv_all[m, seq, :, units:] = (v_acc[m] * m_factor[m]).astype(BF16)
        for k in range(1, n_seq):
            kv_copy(m, k, lax.rem(seq + k, n_seq), seq).start()

        @pl.when(jnp.logical_and(pipe > 0, pipe < last))
        def _():
            enc_copy(m, (pipe + 1, seq, z)).start()

        if wait_q:
            weight_loads[2].wait()

        def project_q(j, carry):
            q_part = (src_cur[m, j].astype(F32) * gain_of(j)).astype(BF16)
            q_acc[m] += dot_nn(q_part, chunk_rows(wq, j))
            return carry

        lax.fori_loop(0, n_mp, project_q, 0)
        for h in range(heads):
            lanes = slice(h * HS, (h + 1) * HS)
            found = q_acc[m, :, lanes] * q_factor[m]
            head = lax.rsqrt(jnp.mean(found * found, axis=-1, keepdims=True) + epsilon)
            q_head[m, h] = head
            queries[m, :, lanes] = (found * head).astype(BF16)

    def forward_b(m):
        for k in range(1, n_seq):
            peer = lax.rem(seq + k, n_seq)
            kv_copy(m, k, peer, peer).wait_recv()
        same = mask[m, my_rows, :]
        for h in range(heads):
            lanes = slice(h * HS, (h + 1) * HS)
            scores = dot_nt(queries[m, :, lanes], keys_of(m, h)) * scale
            weights = jnp.exp(scores) * same
            totals = jnp.sum(weights, axis=-1, keepdims=True)
            summed = dot_nn(weights.astype(BF16), values_of(m, h))
            attended[m, :, lanes] = (summed / totals).astype(BF16)
            portion[m, h] = weights / totals

    def forward_out(m):
        def emit(k, carry):
            j = reduce_order(k)
            block = dot_nn(attended[m], chunk_cols(wo, j))
            reduce_part(0, m, k, j, block, fs_send, fs_relay, fs_copy)
            return carry

        lax.fori_loop(0, n_mp, emit, 0)

    def forward_c(m):
        branch = reduced(m, fs_send, fs_recv, fs_copy)
        updated = (src_cur[m, z].astype(F32) + branch).astype(BF16)
        upd_send[m] = updated

        @pl.when(pipe < last)
        def _():
            for j in hop_order:

                @pl.when(kept(j))
                def _():
                    upd_copy(m, j, z, (pipe + 1, seq, j)).start()

        so_ref[0, m] = updated

    def sort_a(dq, dm):
        return jnp.where(encoder, dq + dm, jnp.where(prev_encoder, dm, dq))

    def sort_b(dq, dm):
        return jnp.where(encoder, 0.0, jnp.where(prev_encoder, dq, dm))

    def to_row(column):
        return jnp.sum(column * eye, axis=0, keepdims=True)

    def to_column(row):
        return jnp.sum(row * eye, axis=1, keepdims=True)

    turns = jnp.logical_and(jnp.logical_not(encoder), prev_encoder)
    first = jnp.logical_or(encoder, prev_encoder)

    def backward_pull(m):
        @pl.when(pipe == last)
        def _():
            def fill(j, carry):
                start = cut(og_ref, m, j).astype(F32)
                u_recv[m, j] = jnp.where(encoder, 0.0, start).astype(BF16)
                return carry

            lax.fori_loop(0, n_mp, fill, 0)
            start = cut(og_ref, m, z).astype(F32)
            gb_recv[m] = jnp.where(encoder, start, 0.0).astype(BF16)

        def pull(k, total):
            j = gather_order(k)

            @pl.when(pipe < last)
            def _():
                u_copy(m, j, j, at_mp(z)).wait_recv()

                @pl.when(jnp.logical_and(is_mid, k == 1))
                def _():
                    pass_copy(1, m, u_recv, u_rsem).start()

            return total + dot_nt(u_recv[m, j], chunk_cols(wo, j))

        d_att[m] = lax.fori_loop(0, n_mp, pull, jnp.zeros((toks, units), F32)).astype(BF16)

    def backward_a(m):
        for h in range(heads):
            lanes = slice(h * HS, (h + 1) * HS)
            wide = slice(units + h * HS, units + (h + 1) * HS)
            probs = portion[m, h]
            pulled = d_att[m, :, lanes]
            along = dot_nt(pulled, values_of(m, h))
            delta = jnp.sum(
                pulled.astype(F32) * attended[m, :, lanes].astype(F32), axis=-1, keepdims=True
            )
            d_scores = (probs * (along - delta)).astype(BF16)
            asked = queries[m, :, lanes]
            value_term = dot_tn(probs.astype(BF16), pulled)
            key_term = dot_tn(d_scores, asked) * scale
            kvg_send[m, :, :, lanes] = key_term.astype(BF16).reshape(n_seq, toks, HS)
            kvg_send[m, :, :, wide] = value_term.astype(BF16).reshape(n_seq, toks, HS)
            d_queries = dot_nn(d_scores, keys_of(m, h)) * scale
            normed = asked.astype(F32)
            mean = jnp.mean(d_queries * normed, axis=-1, keepdims=True)
            q_grad[m, :, lanes] = (q_head[m, h] * (d_queries - normed * mean)).astype(BF16)

        for k in range(1, n_seq):
            kvg_copy(m, k, lax.rem(seq + k, n_seq), seq).start()

        def ask(j, carry):
            dq_buf[m, j] = dot_nt(q_grad[m], chunk_rows(wq, j))
            return carry

        lax.fori_loop(0, n_mp, ask, 0)

    def backward_b(m):
        q_stat = jnp.sum(q_grad[m].astype(F32) * q_acc[m], axis=-1, keepdims=True)
        d_kv = kvg_send[m, seq].astype(F32)
        for k in range(1, n_seq):
            peer = lax.rem(seq + k, n_seq)
            kvg_copy(m, k, peer, peer).wait_recv()
            d_kv = d_kv + kvg_recv[m, peer].astype(F32)
        v_grad[m] = d_kv[:, units:].astype(BF16)
        for h in range(heads):
            lanes = slice(h * HS, (h + 1) * HS)
            d_keys = d_kv[:, lanes]
            normed = kv_all[m, seq, :, lanes].astype(F32)
            mean = jnp.mean(d_keys * normed, axis=-1, keepdims=True)
            k_grad[m, :, lanes] = (k_head[m, h] * (d_keys - normed * mean)).astype(BF16)
        m_stat = jnp.sum(
            k_grad[m].astype(F32) * k_acc[m] + v_grad[m].astype(F32) * v_acc[m],
            axis=-1,
            keepdims=True,
        )
        s_send[m, 0:1, :] = to_row(sort_a(q_stat, m_stat))
        s_send[m, 1:2, :] = to_row(sort_b(q_stat, m_stat))
        s_send[m, 2:, :] = jnp.zeros((6, PAD), F32)
        for k in range(1, n_mp):
            stat_copy(m, lax.rem(z + k, n_mp), z).start()

        def spread_out(k, carry):
            j = reduce_order(k)
            dm = dot_nt(k_grad[m], chunk_rows(wk, j)) + dot_nt(v_grad[m], chunk_rows(wv, j))
            dq = dq_buf[m, j]
            reduce_part(1, m, k, j, sort_a(dq, dm), a_send, a_relay, a_copy)
            b_send[m, j] = sort_b(dq, dm).astype(BF16)
            return carry

        lax.fori_loop(0, n_mp, spread_out, 0)

    def norm_back(values, factor, total, stat):
        return factor * (gain_of(z) * total - values * (factor * factor * (stat / width)))

    def backward_c(m):
        stats = s_send[m]
        for k in range(1, n_mp):
            j = lax.rem(z + k, n_mp)
            stat_copy(m, j, j).wait_recv()
            stats = stats + s_recv[m, j]
        s_total[m] = stats
        total = reduced(m, a_send, a_recv, a_copy)

        @pl.when(pipe < last)
        def _():
            gb_copy(m, at_mp(z)).wait_recv()

        base = jnp.where(turns, gb_recv[m].astype(F32), u_recv[m, z].astype(F32))
        values = jnp.where(turns, enc_cur[m, z].astype(F32), src_cur[m, z].astype(F32))
        factor = jnp.where(turns, m_factor[m], q_factor[m])
        fresh = base + norm_back(values, factor, total, to_column(stats[0:1, :]))
        ahop[m] = fresh.astype(BF16)

        @pl.when(pipe > 0)
        def _():
            for j in hop_order:

                @pl.when(kept(j))
                def _():
                    u_copy(m, j, z, (pipe - 1, seq, j)).start()

    def finish(m, b_new):
        a_new = ahop[m].astype(F32)
        sg_ref[0, 0, m] = jnp.where(first, a_new, b_new).astype(BF16)
        sg_ref[0, 1, m] = jnp.where(first, b_new, a_new).astype(BF16)

    def backward_d(m):
        @pl.when(pipe == 0)
        def _():
            finish(m, gb_recv[m].astype(F32))

        @pl.when(pipe > 0)
        def _():
            total = reduced(m, b_send, b_recv, b_copy)
            base = jnp.where(turns, u_recv[m, z].astype(F32), gb_recv[m].astype(F32))
            values = jnp.where(turns, src_cur[m, z].astype(F32), enc_cur[m, z].astype(F32))
            factor = jnp.where(turns, q_factor[m], m_factor[m])
            fresh = base + norm_back(values, factor, total, to_column(s_total[m, 1:2, :]))
            bhop[m] = fresh.astype(BF16)
            gb_copy(m, (pipe - 1, seq, z)).start()
            finish(m, fresh)

    def backward_rest():
        @pl.when(pipe > 0)
        def _():
            for m in range(batches):
                for j in hop_order:

                    @pl.when(kept(j))
                    def _():
                        u_copy(m, j, z, (pipe - 1, seq, j)).wait_send()

                @pl.when(is_end)
                def _():
                    relay_copy(2, m, b_send, b_relay).start()

                for k in range(1, n_mp):
                    j = lax.rem(z + k, n_mp)
                    held = jnp.logical_and(is_mid, j == other_end)

                    @pl.when(jnp.logical_and(kept(j), jnp.logical_not(held)))
                    def _():
                        b_copy(m, j, z).start()

            @pl.when(is_mid)
            def _():
                for m in range(batches):
                    relay_copy(2, m, b_send, b_relay).wait_recv()
                    joined = b_send[m, other_end].astype(F32) + b_relay[m].astype(F32)
                    b_send[m, other_end] = joined.astype(BF16)
                    b_copy(m, other_end, z).start()

        for m in range(batches):
            backward_d(m)

    @pl.when(pipe < last)
    def _():
        for load in weight_loads[:2]:
            load.wait()
        forward_a(0, True)
        forward_b(0)
        weight_loads[3].wait()
        forward_out(0)
        for m in range(1, batches):
            forward_a(m, False)
            forward_c(m - 1)
            forward_b(m)
            forward_out(m)
        forward_c(batches - 1)
        backward_pull(0)
        backward_a(0)
        backward_b(0)
        for m in range(1, batches):
            backward_pull(m)
            backward_a(m)
            backward_c(m - 1)
            backward_b(m)
        backward_c(batches - 1)
        backward_rest()

    @pl.when(pipe == last)
    def _():
        for load in weight_loads:
            load.wait()
        for m in range(batches):
            backward_pull(m)
        forward_a(0, False)
        forward_b(0)
        backward_a(0)
        backward_b(0)
        for m in range(1, batches):
            forward_a(m, False)
            backward_c(m - 1)
            forward_b(m)
            backward_a(m)
            backward_b(m)
        backward_c(batches - 1)
        backward_rest()
        for m in range(batches):
            forward_out(m)
        for m in range(batches):
            forward_c(m)

    @pl.when(jnp.logical_and(pipe > 0, pipe < last))
    def _():
        for m in range(batches):
            enc_copy(m, (pipe + 1, seq, z)).wait_send()

    for m in range(batches):
        for k in range(1, n_seq):
            peer = lax.rem(seq + k, n_seq)
            kv_copy(m, k, peer, seq).wait_send()
            kvg_copy(m, k, peer, seq).wait_send()
        for k in range(1, n_mp):
            j = lax.rem(z + k, n_mp)
            stat_copy(m, j, z).wait_send()
        reduce_drain(0, m, fs_send, fs_relay, fs_copy)
        reduce_drain(1, m, a_send, a_relay, a_copy)

    @pl.when(pipe < last)
    def _():
        for m in range(batches):
            for j in hop_order:

                @pl.when(kept(j))
                def _():
                    upd_copy(m, j, z, (pipe + 1, seq, j)).wait_send()

            @pl.when(is_mid)
            def _():
                pass_copy(1, m, u_recv, u_rsem).wait_send()

    @pl.when(pipe > 0)
    def _():
        for m in range(batches):
            gb_copy(m, (pipe - 1, seq, z)).wait_send()
            reduce_drain(2, m, b_send, b_relay, b_copy)

            @pl.when(is_mid)
            def _():
                pass_copy(0, m, upd_recv, upd_rsem).wait_send()


def per_device(n_pipe, n_seq, n_mp, enc_in, dec_in, doc_ids, enc_sections, norm_gain,
               q_weight, k_weight, v_weight, o_weight, out_grad):
    batches, toks, width = enc_in.shape
    share = width // n_mp
    heads = HEADS // n_mp
    units = heads * HS
    length = n_seq * toks
    vmem = pl.BlockSpec(memory_space=pltpu.VMEM)
    hbm = pl.BlockSpec(memory_space=pl.ANY)
    smem = pl.BlockSpec(memory_space=pltpu.SMEM)
    V = pltpu.VMEM
    dma = pltpu.SemaphoreType.DMA
    scratch = [
        V((width, units), BF16),
        V((width, units), BF16),
        V((width, units), BF16),
        V((units, width), BF16),
        dma((4,)),
        V((batches, length, length), F32),
        V((batches, n_mp, toks, share), BF16),
        V((batches, n_mp, toks, share), BF16),
        V((batches, n_mp, toks, share), BF16),
        V((batches, n_mp, toks, share), BF16),
        V((batches, toks, units), F32),
        V((batches, toks, units), F32),
        V((batches, toks, units), F32),
        V((batches, toks, units), BF16),
        V((batches, toks, 1), F32),
        V((batches, toks, 1), F32),
        V((batches, heads, toks, 1), F32),
        V((batches, heads, toks, 1), F32),
        V((batches, n_seq, toks, 2 * units), BF16),
        V((batches, heads, toks, length), F32),
        V((batches, toks, units), BF16),
        V((batches, n_mp, toks, share), BF16),
        V((batches, n_mp, toks, share), BF16),
        V((batches, toks, share), BF16),
        V((batches, n_mp, toks, share), BF16),
        V((batches, toks, units), BF16),
        V((batches, n_seq, toks, 2 * units), BF16),
        V((batches, n_seq, toks, 2 * units), BF16),
        V((batches, toks, units), BF16),
        V((batches, toks, units), BF16),
        V((batches, toks, units), BF16),
        V((batches, n_mp, toks, share), F32),
        V((batches, n_mp, toks, share), BF16),
        V((batches, n_mp, toks, share), BF16),
        V((batches, n_mp, toks, share), BF16),
        V((batches, n_mp, toks, share), BF16),
        V((batches, 8, PAD), F32),
        V((batches, n_mp, 8, PAD), F32),
        V((batches, 8, PAD), F32),
        V((batches, toks, share), BF16),
        V((batches, toks, share), BF16),
        V((batches, toks, share), BF16),
        V((batches, toks, share), BF16),
        V((batches, toks, share), BF16),
        V((batches, toks, share), BF16),
        dma((batches, n_mp)),
        dma((batches, n_mp)),
        dma((batches,)),
        dma((batches,)),
        dma((batches, n_seq)),
        dma((batches, n_seq)),
        dma((batches, n_mp)),
        dma((batches, n_mp)),
        dma((batches, n_mp)),
        dma((batches, n_mp)),
        dma((batches, n_seq)),
        dma((batches, n_seq)),
        dma((batches, n_mp)),
        dma((batches, n_mp)),
        dma((batches, n_mp)),
        dma((batches, n_mp)),
        dma((batches, n_mp)),
        dma((batches, n_mp)),
        dma((3, batches)),
        dma((3, batches)),
        dma((2, batches)),
        dma((batches,)),
        dma((batches,)),
    ]
    return pl.pallas_call(
        functools.partial(kernel, n_pipe, n_seq, n_mp),
        out_shape=(
            jax.ShapeDtypeStruct((1, batches, toks, share), BF16),
            jax.ShapeDtypeStruct((1, 2, batches, toks, share), BF16),
        ),
        in_specs=[vmem, vmem, vmem, smem, vmem, hbm, hbm, hbm, hbm, vmem],
        out_specs=(vmem, vmem),
        scratch_shapes=scratch,
        compiler_params=pltpu.CompilerParams(
            collective_id=0, has_side_effects=True, vmem_limit_bytes=56 * 1024 * 1024
        ),
    )(enc_in, dec_in, doc_ids, enc_sections, norm_gain, q_weight, k_weight, v_weight, o_weight,
      out_grad)


def solution(mesh):
    sizes = (mesh.shape["pipe"], mesh.shape["seq"], mesh.shape["mp"])
    return jax.shard_map(
        functools.partial(per_device, *sizes),
        mesh=mesh,
        in_specs=(
            P(None, "seq", None),
            P(None, "seq", None),
            P(),
            P(),
            P("pipe", None),
            P("pipe", None, "mp"),
            P("pipe", None, "mp"),
            P("pipe", None, "mp"),
            P("pipe", "mp", None),
            P(None, "seq", None),
        ),
        out_specs=(P("pipe", None, "seq", "mp"), P("pipe", None, None, "seq", "mp")),
        check_vma=False,
    )
```

```python
import functools

import jax
import jax.numpy as jnp
from jax import lax
from jax.experimental import pallas as pl
from jax.experimental.pallas import tpu as pltpu
from jax.sharding import PartitionSpec as P

HEADS = 8
HS = 256
PAD = 128
SPLIT = 2

epsilon = 1e-06
MESH = pl.DeviceIdType.MESH
F32 = jnp.float32
BF16 = jnp.bfloat16


def dot_nn(a, b):
    return jnp.dot(a, b, preferred_element_type=F32)


def dot_nt(a, b):
    return lax.dot_general(a, b, (((1,), (1,)), ((), ())), preferred_element_type=F32)


def dot_tn(a, b):
    return lax.dot_general(a, b, (((0,), (0,)), ((), ())), preferred_element_type=F32)


def kernel(
    n_pipe,
    n_seq,
    n_mp,
    enc_ref,
    dec_ref,
    doc_ref,
    count_ref,
    gain_ref,
    wq_hbm,
    wk_hbm,
    wv_hbm,
    wo_hbm,
    og_ref,
    so_ref,
    sg_ref,
    wq,
    wk,
    wv,
    wo,
    w_sem,
    mask,
    upd_recv,
    enc_recv,
    enc_cur,
    src_cur,
    q_acc,
    k_acc,
    v_acc,
    queries,
    q_factor,
    m_factor,
    q_head,
    k_head,
    kv_all,
    portion,
    attended,
    fs_send,
    fs_recv,
    upd_send,
    u_recv,
    d_att,
    kvg_send,
    kvg_recv,
    q_grad,
    k_grad,
    v_grad,
    dq_buf,
    a_send,
    a_recv,
    b_send,
    b_recv,
    s_send,
    s_recv,
    s_total,
    fs_relay,
    a_relay,
    b_relay,
    ahop,
    bhop,
    gb_recv,
    upd_ssem,
    upd_rsem,
    enc_ssem,
    enc_rsem,
    kv_ssem,
    kv_rsem,
    fs_ssem,
    fs_rsem,
    u_ssem,
    u_rsem,
    kvg_ssem,
    kvg_rsem,
    a_ssem,
    a_rsem,
    b_ssem,
    b_rsem,
    s_ssem,
    s_rsem,
    relay_ssem,
    relay_rsem,
    pass_ssem,
    gb_ssem,
    gb_rsem,
    clear_sem,
):
    pipe = lax.axis_index("pipe")
    seq = lax.axis_index("seq")
    z = lax.axis_index("mp")
    batches, toks, width = enc_ref.shape
    share = width // n_mp
    part = share // SPLIT
    heads = HEADS // n_mp
    units = heads * HS
    scale = HS ** (-0.5)
    last = n_pipe - 1

    def at_mp(j):
        return (pipe, seq, j)

    def at_seq(i):
        return (pipe, i, z)

    def copy(src, dst, ssem, rsem, device):
        return pltpu.make_async_remote_copy(
            src_ref=src,
            dst_ref=dst,
            send_sem=ssem,
            recv_sem=rsem,
            device_id=device,
            device_id_type=MESH,
        )

    weight_loads = [
        pltpu.make_async_copy(hbm.at[0], vmem, w_sem.at[i])
        for i, (hbm, vmem) in enumerate(
            [(wk_hbm, wk), (wv_hbm, wv), (wq_hbm, wq), (wo_hbm, wo)]
        )
    ]
    for load in weight_loads:
        load.start()

    barrier = pltpu.get_barrier_semaphore()
    for k in range(1, n_mp):
        pl.semaphore_signal(
            barrier, inc=1, device_id=at_mp(lax.rem(z + k, n_mp)), device_id_type=MESH
        )
    for k in range(1, n_seq):
        pl.semaphore_signal(
            barrier, inc=1, device_id=at_seq(lax.rem(seq + k, n_seq)), device_id_type=MESH
        )

    @pl.when(pipe > 0)
    def _():
        for j in range(n_mp):
            pl.semaphore_signal(
                barrier, inc=1, device_id=(pipe - 1, seq, j), device_id_type=MESH
            )

    @pl.when(pipe < last)
    def _():
        for j in range(n_mp):
            pl.semaphore_signal(
                barrier, inc=1, device_id=(pipe + 1, seq, j), device_id_type=MESH
            )

    edge = jnp.where(pipe > 0, n_mp, 0) + jnp.where(pipe < last, n_mp, 0)
    pl.semaphore_wait(barrier, n_mp - 1 + n_seq - 1 + edge)

    encoder = pipe < count_ref[0]
    prev_encoder = pipe - 1 < count_ref[0]

    def span(f, j):
        return pl.ds(pl.multiple_of(j * share + f * part, part), part)

    def cut(ref, m, f, j):
        return ref[m, :, span(f, j)]

    def gain_of(f, j):
        return gain_ref[:, span(f, j)]

    def chunk_rows(ref, f, j):
        return ref[span(f, j), :]

    def chunk_cols(ref, f, j):
        return ref[:, span(f, j)]

    def slabs(m):
        return pl.ds(m * SPLIT, SPLIT)

    pieces = SPLIT * n_mp

    def piece(i):
        return lax.div(i, n_mp), lax.rem(i, n_mp)

    length = n_seq * toks
    for m in range(batches):
        row = doc_ref[m : m + 1, :].astype(F32)
        spread = jnp.broadcast_to(row, (length, length))
        mask[m] = (spread == spread.T).astype(F32)
    eye = (
        lax.broadcasted_iota(jnp.int32, (toks, PAD), 0)
        == lax.broadcasted_iota(jnp.int32, (toks, PAD), 1)
    ).astype(F32)
    my_rows = pl.ds(pl.multiple_of(seq * toks, toks), toks)
    none = jnp.zeros((toks, 1), F32)

    def keys_of(m, h):
        return kv_all[m, :, :, h * HS : (h + 1) * HS].reshape(length, HS)

    def values_of(m, h):
        return kv_all[m, :, :, units + h * HS : units + (h + 1) * HS].reshape(length, HS)

    def enc_copy(m, device):
        return copy(enc_cur.at[slabs(m)], enc_recv.at[slabs(m)], enc_ssem.at[m], enc_rsem.at[m], device)

    def kv_copy(m, slot, peer, owner):
        return copy(
            kv_all.at[m, seq], kv_all.at[m, owner], kv_ssem.at[m, slot], kv_rsem.at[m, owner],
            at_seq(peer),
        )

    def kvg_copy(m, slot, peer, owner):
        return copy(
            kvg_send.at[m, peer], kvg_recv.at[m, owner], kvg_ssem.at[m, slot],
            kvg_rsem.at[m, owner], at_seq(peer),
        )

    def fs_copy(m, j, owner):
        return copy(
            fs_send.at[m, j], fs_recv.at[m, owner], fs_ssem.at[m, j], fs_rsem.at[m, owner],
            at_mp(j),
        )

    def upd_copy(m, j, owner, device):
        return copy(
            upd_send.at[m], upd_recv.at[m, owner], upd_ssem.at[m, j], upd_rsem.at[m, owner],
            device,
        )

    def u_copy(m, j, owner, device):
        return copy(
            ahop.at[m], u_recv.at[m, owner], u_ssem.at[m, j], u_rsem.at[m, owner], device
        )

    def stat_copy(m, j, owner):
        return copy(
            s_send.at[m], s_recv.at[m, owner], s_ssem.at[m, j], s_rsem.at[m, owner], at_mp(j)
        )

    def a_copy(m, j, owner):
        return copy(
            a_send.at[m, j], a_recv.at[m, owner], a_ssem.at[m, j], a_rsem.at[m, owner], at_mp(j)
        )

    def b_copy(m, j, owner):
        return copy(
            b_send.at[m, j], b_recv.at[m, owner], b_ssem.at[m, j], b_rsem.at[m, owner], at_mp(j)
        )

    def gb_copy(m, device):
        return copy(
            bhop.at[slabs(m)], gb_recv.at[slabs(m)], gb_ssem.at[m], gb_rsem.at[m], device
        )

    chain = n_mp == 4
    far = n_mp - 1 - z
    upper = z >= n_mp // 2
    near_z = jnp.where(upper, far, z)
    is_end = near_z == 0 if chain else z < 0
    is_mid = near_z == 1 if chain else z < 0
    partner = jnp.where(upper, n_mp - 2, 1)
    other_end = jnp.where(upper, 0, n_mp - 1)
    this_end = jnp.where(upper, n_mp - 1, 0)

    def mirror(j):
        return jnp.where(upper, n_mp - 1 - j, j)

    def reduce_order(k):
        if not chain:
            return lax.rem(z + 1 + k, n_mp)
        mid = jnp.where(k == 0, 2, jnp.where(k == 3, 3, k - 1))
        return mirror(jnp.where(is_end, 3 - k, mid))

    def gather_order(k):
        if not chain:
            return lax.rem(z + k, n_mp)
        mid = jnp.where(k == 0, 1, jnp.where(k == 1, 3, jnp.where(k == 2, 0, 2)))
        return mirror(jnp.where(is_end, k, mid))

    def skipped(j):
        return jnp.logical_and(is_end, j == far)

    def kept(j):
        return jnp.logical_not(skipped(j))

    def relay_copy(which, m, send, relay):
        return copy(
            send.at[m, far], relay.at[m], relay_ssem.at[which, m], relay_rsem.at[which, m],
            at_mp(partner),
        )

    def pass_copy(which, m, buffer, rsem):
        return copy(
            buffer.at[m, other_end], buffer.at[m, other_end], pass_ssem.at[which, m],
            rsem.at[m, other_end], at_mp(this_end),
        )

    def reduce_part(which, m, k, j, block, send, relay, direct):
        send[m, j] = block.astype(BF16)
        closing = jnp.logical_and(is_mid, k == n_mp - 1)
        opening = jnp.logical_and(is_end, k == 0)

        @pl.when(closing)
        def _():
            relay_copy(which, m, send, relay).wait_recv()
            send[m, j] = (block + relay[m].astype(F32)).astype(BF16)

        @pl.when(opening)
        def _():
            relay_copy(which, m, send, relay).start()

        @pl.when(jnp.logical_and(j != z, kept(j)))
        def _():
            direct(m, j, z).start()

    def reduced(m, send, recv, direct):
        total = send[m, z].astype(F32)
        for k in range(1, n_mp):
            j = lax.rem(z + k, n_mp)

            @pl.when(kept(j))
            def _():
                direct(m, j, j).wait_recv()

            total = total + recv[m, j].astype(F32)
        return total

    def reduce_drain(which, m, send, relay, direct):
        for k in range(1, n_mp):
            j = lax.rem(z + k, n_mp)

            @pl.when(kept(j))
            def _():
                direct(m, j, z).wait_send()

        @pl.when(is_end)
        def _():
            relay_copy(which, m, send, relay).wait_send()

    @pl.when(is_end)
    def _():
        for p in range(batches * SPLIT):
            for recv in (fs_recv, a_recv, b_recv):
                recv[p, far] = jnp.zeros((toks, part), BF16)

    hop_order = [lax.rem(z + k, n_mp) for k in sorted(range(n_mp), key=lambda k: (k == 0, k != 2))]

    def forward_a(m, wait_q):
        @pl.when(pipe == 0)
        def _():
            def fill(i, carry):
                f, j = piece(i)
                upd_recv[m * SPLIT + f, j] = cut(enc_ref, m, f, j)
                return carry

            lax.fori_loop(0, pieces, fill, 0)

        @pl.when(pipe > 1)
        def _():
            enc_copy(m, at_mp(z)).wait_recv()

        k_acc[m] = jnp.zeros((toks, units), F32)
        v_acc[m] = jnp.zeros((toks, units), F32)
        q_acc[m] = jnp.zeros((toks, units), F32)

        def project(i, sums):
            f, k = piece(i)
            j = gather_order(k)
            p = m * SPLIT + f

            @pl.when(pipe > 0)
            def _():
                upd_copy(p, j, j, at_mp(z)).wait_recv()

                @pl.when(jnp.logical_and(is_mid, k == 1))
                def _():
                    pass_copy(0, p, upd_recv, upd_rsem).start()

            fresh = upd_recv[p, j].astype(F32)
            enc = jnp.where(prev_encoder, fresh, enc_recv[p, j].astype(F32))
            dec = jnp.where(prev_encoder, cut(dec_ref, m, f, j).astype(F32), fresh)
            src = jnp.where(encoder, enc, dec)
            enc_cur[p, j] = enc.astype(BF16)
            src_cur[p, j] = src.astype(BF16)
            m_part = (enc * gain_of(f, j)).astype(BF16)
            k_acc[m] += dot_nn(m_part, chunk_rows(wk, f, j))
            v_acc[m] += dot_nn(m_part, chunk_rows(wv, f, j))
            return (
                sums[0] + jnp.sum(src * src, axis=-1, keepdims=True),
                sums[1] + jnp.sum(enc * enc, axis=-1, keepdims=True),
            )

        q_square, m_square = lax.fori_loop(0, pieces, project, (none, none))
        q_factor[m] = lax.rsqrt(q_square / width + epsilon)
        m_factor[m] = lax.rsqrt(m_square / width + epsilon)

        for h in range(heads):
            lanes = slice(h * HS, (h + 1) * HS)
            keys = k_acc[m, :, lanes] * m_factor[m]
            head = lax.rsqrt(jnp.mean(keys * keys, axis=-1, keepdims=True) + epsilon)
            k_head[m, h] = head
            kv_all[m, seq, :, lanes] = (keys * head).astype(BF16)
        kv_all[m, seq, :, units:] = (v_acc[m] * m_factor[m]).astype(BF16)
        for k in range(1, n_seq):
            kv_copy(m, k, lax.rem(seq + k, n_seq), seq).start()

        @pl.when(jnp.logical_and(pipe > 0, pipe < last))
        def _():
            enc_copy(m, (pipe + 1, seq, z)).start()

        if wait_q:
            weight_loads[2].wait()

        def project_q(i, carry):
            f, j = piece(i)
            q_part = (src_cur[m * SPLIT + f, j].astype(F32) * gain_of(f, j)).astype(BF16)
            q_acc[m] += dot_nn(q_part, chunk_rows(wq, f, j))
            return carry

        lax.fori_loop(0, pieces, project_q, 0)
        for h in range(heads):
            lanes = slice(h * HS, (h + 1) * HS)
            found = q_acc[m, :, lanes] * q_factor[m]
            head = lax.rsqrt(jnp.mean(found * found, axis=-1, keepdims=True) + epsilon)
            q_head[m, h] = head
            queries[m, :, lanes] = (found * head).astype(BF16)

    def forward_b(m):
        for k in range(1, n_seq):
            peer = lax.rem(seq + k, n_seq)
            kv_copy(m, k, peer, peer).wait_recv()
        same = mask[m, my_rows, :]
        for h in range(heads):
            lanes = slice(h * HS, (h + 1) * HS)
            scores = dot_nt(queries[m, :, lanes], keys_of(m, h)) * scale
            weights = jnp.exp(scores) * same
            totals = jnp.sum(weights, axis=-1, keepdims=True)
            summed = dot_nn(weights.astype(BF16), values_of(m, h))
            attended[m, :, lanes] = (summed / totals).astype(BF16)
            portion[m, h] = weights / totals

    def forward_out(m):
        def emit(i, carry):
            f, k = piece(i)
            j = reduce_order(k)
            block = dot_nn(attended[m], chunk_cols(wo, f, j))
            reduce_part(0, m * SPLIT + f, k, j, block, fs_send, fs_relay, fs_copy)
            return carry

        lax.fori_loop(0, pieces, emit, 0)

    def forward_c(m):
        for f in range(SPLIT):
            p = m * SPLIT + f
            branch = reduced(p, fs_send, fs_recv, fs_copy)
            updated = (src_cur[p, z].astype(F32) + branch).astype(BF16)
            upd_send[p] = updated

            @pl.when(pipe < last)
            def _():
                for j in hop_order:

                    @pl.when(kept(j))
                    def _():
                        upd_copy(p, j, z, (pipe + 1, seq, j)).start()

            so_ref[0, m, :, f * part : (f + 1) * part] = updated

    def sort_a(dq, dm):
        return jnp.where(encoder, dq + dm, jnp.where(prev_encoder, dm, dq))

    def sort_b(dq, dm):
        return jnp.where(encoder, 0.0, jnp.where(prev_encoder, dq, dm))

    def to_row(column):
        return jnp.sum(column * eye, axis=0, keepdims=True)

    def to_column(row):
        return jnp.sum(row * eye, axis=1, keepdims=True)

    turns = jnp.logical_and(jnp.logical_not(encoder), prev_encoder)
    first = jnp.logical_or(encoder, prev_encoder)

    def backward_pull(m):
        @pl.when(pipe == last)
        def _():
            def fill(i, carry):
                f, j = piece(i)
                start = cut(og_ref, m, f, j).astype(F32)
                u_recv[m * SPLIT + f, j] = jnp.where(encoder, 0.0, start).astype(BF16)
                return carry

            lax.fori_loop(0, pieces, fill, 0)
            for f in range(SPLIT):
                start = cut(og_ref, m, f, z).astype(F32)
                gb_recv[m * SPLIT + f] = jnp.where(encoder, start, 0.0).astype(BF16)

        def pull(i, total):
            f, k = piece(i)
            j = gather_order(k)
            p = m * SPLIT + f

            @pl.when(pipe < last)
            def _():
                u_copy(p, j, j, at_mp(z)).wait_recv()

                @pl.when(jnp.logical_and(is_mid, k == 1))
                def _():
                    pass_copy(1, p, u_recv, u_rsem).start()

            return total + dot_nt(u_recv[p, j], chunk_cols(wo, f, j))

        d_att[m] = lax.fori_loop(
            0, pieces, pull, jnp.zeros((toks, units), F32)).astype(BF16)

    def backward_a(m):
        for h in range(heads):
            lanes = slice(h * HS, (h + 1) * HS)
            wide = slice(units + h * HS, units + (h + 1) * HS)
            probs = portion[m, h]
            pulled = d_att[m, :, lanes]
            along = dot_nt(pulled, values_of(m, h))
            delta = jnp.sum(
                pulled.astype(F32) * attended[m, :, lanes].astype(F32), axis=-1, keepdims=True
            )
            d_scores = (probs * (along - delta)).astype(BF16)
            asked = queries[m, :, lanes]
            value_term = dot_tn(probs.astype(BF16), pulled)
            key_term = dot_tn(d_scores, asked) * scale
            kvg_send[m, :, :, lanes] = key_term.astype(BF16).reshape(n_seq, toks, HS)
            kvg_send[m, :, :, wide] = value_term.astype(BF16).reshape(n_seq, toks, HS)
            d_queries = dot_nn(d_scores, keys_of(m, h)) * scale
            normed = asked.astype(F32)
            mean = jnp.mean(d_queries * normed, axis=-1, keepdims=True)
            q_grad[m, :, lanes] = (q_head[m, h] * (d_queries - normed * mean)).astype(BF16)

        for k in range(1, n_seq):
            kvg_copy(m, k, lax.rem(seq + k, n_seq), seq).start()

        def ask(i, carry):
            f, j = piece(i)
            dq_buf[m * SPLIT + f, j] = dot_nt(q_grad[m], chunk_rows(wq, f, j))
            return carry

        lax.fori_loop(0, pieces, ask, 0)

    def backward_b(m):
        q_stat = jnp.sum(q_grad[m].astype(F32) * q_acc[m], axis=-1, keepdims=True)
        d_kv = kvg_send[m, seq].astype(F32)
        for k in range(1, n_seq):
            peer = lax.rem(seq + k, n_seq)
            kvg_copy(m, k, peer, peer).wait_recv()
            d_kv = d_kv + kvg_recv[m, peer].astype(F32)
        v_grad[m] = d_kv[:, units:].astype(BF16)
        for h in range(heads):
            lanes = slice(h * HS, (h + 1) * HS)
            d_keys = d_kv[:, lanes]
            normed = kv_all[m, seq, :, lanes].astype(F32)
            mean = jnp.mean(d_keys * normed, axis=-1, keepdims=True)
            k_grad[m, :, lanes] = (k_head[m, h] * (d_keys - normed * mean)).astype(BF16)
        m_stat = jnp.sum(
            k_grad[m].astype(F32) * k_acc[m] + v_grad[m].astype(F32) * v_acc[m],
            axis=-1,
            keepdims=True,
        )
        s_send[m, 0:1, :] = to_row(sort_a(q_stat, m_stat))
        s_send[m, 1:2, :] = to_row(sort_b(q_stat, m_stat))
        s_send[m, 2:, :] = jnp.zeros((6, PAD), F32)
        for k in range(1, n_mp):
            stat_copy(m, lax.rem(z + k, n_mp), z).start()

        def spread_out(i, carry):
            f, k = piece(i)
            p = m * SPLIT + f
            j = reduce_order(k)
            dm = dot_nt(k_grad[m], chunk_rows(wk, f, j)) + dot_nt(v_grad[m], chunk_rows(wv, f, j))
            dq = dq_buf[p, j]
            reduce_part(1, p, k, j, sort_a(dq, dm), a_send, a_relay, a_copy)
            b_send[p, j] = sort_b(dq, dm).astype(BF16)
            return carry

        lax.fori_loop(0, pieces, spread_out, 0)

    def norm_back(f, values, factor, total, stat):
        return factor * (gain_of(f, z) * total - values * (factor * factor * (stat / width)))

    def backward_c(m):
        stats = s_send[m]
        for k in range(1, n_mp):
            j = lax.rem(z + k, n_mp)
            stat_copy(m, j, j).wait_recv()
            stats = stats + s_recv[m, j]
        s_total[m] = stats
        factor = jnp.where(turns, m_factor[m], q_factor[m])
        stat = to_column(stats[0:1, :])
        for f in range(SPLIT):
            p = m * SPLIT + f
            total = reduced(p, a_send, a_recv, a_copy)
            if f == 0:

                @pl.when(pipe < last)
                def _():
                    gb_copy(m, at_mp(z)).wait_recv()

            base = jnp.where(turns, gb_recv[p].astype(F32), u_recv[p, z].astype(F32))
            values = jnp.where(turns, enc_cur[p, z].astype(F32), src_cur[p, z].astype(F32))
            fresh = base + norm_back(f, values, factor, total, stat)
            ahop[p] = fresh.astype(BF16)

            @pl.when(pipe > 0)
            def _():
                for j in hop_order:

                    @pl.when(kept(j))
                    def _():
                        u_copy(p, j, z, (pipe - 1, seq, j)).start()

    def finish(m, f, b_new):
        a_new = ahop[m * SPLIT + f].astype(F32)
        lanes = slice(f * part, (f + 1) * part)
        sg_ref[0, 0, m, :, lanes] = jnp.where(first, a_new, b_new).astype(BF16)
        sg_ref[0, 1, m, :, lanes] = jnp.where(first, b_new, a_new).astype(BF16)

    def backward_d(m):
        @pl.when(pipe == 0)
        def _():
            for f in range(SPLIT):
                finish(m, f, gb_recv[m * SPLIT + f].astype(F32))

        @pl.when(pipe > 0)
        def _():
            factor = jnp.where(turns, q_factor[m], m_factor[m])
            stat = to_column(s_total[m, 1:2, :])
            for f in range(SPLIT):
                p = m * SPLIT + f
                total = reduced(p, b_send, b_recv, b_copy)
                base = jnp.where(turns, u_recv[p, z].astype(F32), gb_recv[p].astype(F32))
                values = jnp.where(turns, src_cur[p, z].astype(F32), enc_cur[p, z].astype(F32))
                fresh = base + norm_back(f, values, factor, total, stat)
                bhop[p] = fresh.astype(BF16)
                finish(m, f, fresh)
            gb_copy(m, (pipe - 1, seq, z)).start()

    def backward_rest():
        @pl.when(pipe > 0)
        def _():
            for m in range(batches * SPLIT):
                for j in hop_order:

                    @pl.when(kept(j))
                    def _():
                        u_copy(m, j, z, (pipe - 1, seq, j)).wait_send()

                @pl.when(is_end)
                def _():
                    relay_copy(2, m, b_send, b_relay).start()

                for k in range(1, n_mp):
                    j = lax.rem(z + k, n_mp)
                    held = jnp.logical_and(is_mid, j == other_end)

                    @pl.when(jnp.logical_and(kept(j), jnp.logical_not(held)))
                    def _():
                        b_copy(m, j, z).start()

            @pl.when(is_mid)
            def _():
                for m in range(batches * SPLIT):
                    relay_copy(2, m, b_send, b_relay).wait_recv()
                    joined = b_send[m, other_end].astype(F32) + b_relay[m].astype(F32)
                    b_send[m, other_end] = joined.astype(BF16)
                    b_copy(m, other_end, z).start()

        for m in range(batches):
            backward_d(m)

    @pl.when(pipe < last)
    def _():
        for load in weight_loads[:2]:
            load.wait()
        forward_a(0, True)
        forward_b(0)
        weight_loads[3].wait()
        forward_out(0)
        for m in range(1, batches):
            forward_a(m, False)
            forward_c(m - 1)
            forward_b(m)
            forward_out(m)
        forward_c(batches - 1)
        backward_pull(0)
        backward_a(0)
        backward_b(0)
        for m in range(1, batches):
            backward_pull(m)
            backward_a(m)
            backward_c(m - 1)
            backward_b(m)
        backward_c(batches - 1)
        backward_rest()

        @pl.when(pipe == last - 1)
        def _():
            pl.semaphore_signal(
                clear_sem, inc=1, device_id=(pipe + 1, seq, z), device_id_type=MESH
            )

    @pl.when(pipe == last)
    def _():
        for load in weight_loads:
            load.wait()
        for m in range(batches):
            backward_pull(m)
        forward_a(0, False)
        forward_b(0)
        backward_a(0)
        backward_b(0)
        for m in range(1, batches):
            forward_a(m, False)
            backward_c(m - 1)
            forward_b(m)
            backward_a(m)
            backward_b(m)
        backward_c(batches - 1)
        backward_rest()
        if last > 0:
            pl.semaphore_wait(clear_sem, 1)
        for m in range(batches):
            forward_out(m)
        for m in range(batches):
            forward_c(m)

    @pl.when(jnp.logical_and(pipe > 0, pipe < last))
    def _():
        for m in range(batches):
            enc_copy(m, (pipe + 1, seq, z)).wait_send()

    for m in range(batches):
        for k in range(1, n_seq):
            peer = lax.rem(seq + k, n_seq)
            kv_copy(m, k, peer, seq).wait_send()
            kvg_copy(m, k, peer, seq).wait_send()
        for k in range(1, n_mp):
            stat_copy(m, lax.rem(z + k, n_mp), z).wait_send()
    for p in range(batches * SPLIT):
        reduce_drain(0, p, fs_send, fs_relay, fs_copy)
        reduce_drain(1, p, a_send, a_relay, a_copy)

    @pl.when(pipe < last)
    def _():
        for p in range(batches * SPLIT):
            for j in hop_order:

                @pl.when(kept(j))
                def _():
                    upd_copy(p, j, z, (pipe + 1, seq, j)).wait_send()

            @pl.when(is_mid)
            def _():
                pass_copy(1, p, u_recv, u_rsem).wait_send()

    @pl.when(pipe > 0)
    def _():
        for m in range(batches):
            gb_copy(m, (pipe - 1, seq, z)).wait_send()
        for p in range(batches * SPLIT):
            reduce_drain(2, p, b_send, b_relay, b_copy)

            @pl.when(is_mid)
            def _():
                pass_copy(0, p, upd_recv, upd_rsem).wait_send()


def per_device(n_pipe, n_seq, n_mp, enc_in, dec_in, doc_ids, enc_sections, norm_gain,
               q_weight, k_weight, v_weight, o_weight, out_grad):
    batches, toks, width = enc_in.shape
    share = width // n_mp
    part = share // SPLIT
    heads = HEADS // n_mp
    units = heads * HS
    length = n_seq * toks
    vmem = pl.BlockSpec(memory_space=pltpu.VMEM)
    hbm = pl.BlockSpec(memory_space=pl.ANY)
    smem = pl.BlockSpec(memory_space=pltpu.SMEM)
    V = pltpu.VMEM
    dma = pltpu.SemaphoreType.DMA
    scratch = [
        V((width, units), BF16),
        V((width, units), BF16),
        V((width, units), BF16),
        V((units, width), BF16),
        dma((4,)),
        V((batches, length, length), F32),
        V((batches * SPLIT, n_mp, toks, part), BF16),
        V((batches * SPLIT, n_mp, toks, part), BF16),
        V((batches * SPLIT, n_mp, toks, part), BF16),
        V((batches * SPLIT, n_mp, toks, part), BF16),
        V((batches, toks, units), F32),
        V((batches, toks, units), F32),
        V((batches, toks, units), F32),
        V((batches, toks, units), BF16),
        V((batches, toks, 1), F32),
        V((batches, toks, 1), F32),
        V((batches, heads, toks, 1), F32),
        V((batches, heads, toks, 1), F32),
        V((batches, n_seq, toks, 2 * units), BF16),
        V((batches, heads, toks, length), F32),
        V((batches, toks, units), BF16),
        V((batches * SPLIT, n_mp, toks, part), BF16),
        V((batches * SPLIT, n_mp, toks, part), BF16),
        V((batches * SPLIT, toks, part), BF16),
        V((batches * SPLIT, n_mp, toks, part), BF16),
        V((batches, toks, units), BF16),
        V((batches, n_seq, toks, 2 * units), BF16),
        V((batches, n_seq, toks, 2 * units), BF16),
        V((batches, toks, units), BF16),
        V((batches, toks, units), BF16),
        V((batches, toks, units), BF16),
        V((batches * SPLIT, n_mp, toks, part), F32),
        V((batches * SPLIT, n_mp, toks, part), BF16),
        V((batches * SPLIT, n_mp, toks, part), BF16),
        V((batches * SPLIT, n_mp, toks, part), BF16),
        V((batches * SPLIT, n_mp, toks, part), BF16),
        V((batches, 8, PAD), F32),
        V((batches, n_mp, 8, PAD), F32),
        V((batches, 8, PAD), F32),
        V((batches * SPLIT, toks, part), BF16),
        V((batches * SPLIT, toks, part), BF16),
        V((batches * SPLIT, toks, part), BF16),
        V((batches * SPLIT, toks, part), BF16),
        V((batches * SPLIT, toks, part), BF16),
        V((batches * SPLIT, toks, part), BF16),
        dma((batches * SPLIT, n_mp)),
        dma((batches * SPLIT, n_mp)),
        dma((batches,)),
        dma((batches,)),
        dma((batches, n_seq)),
        dma((batches, n_seq)),
        dma((batches * SPLIT, n_mp)),
        dma((batches * SPLIT, n_mp)),
        dma((batches * SPLIT, n_mp)),
        dma((batches * SPLIT, n_mp)),
        dma((batches, n_seq)),
        dma((batches, n_seq)),
        dma((batches * SPLIT, n_mp)),
        dma((batches * SPLIT, n_mp)),
        dma((batches * SPLIT, n_mp)),
        dma((batches * SPLIT, n_mp)),
        dma((batches, n_mp)),
        dma((batches, n_mp)),
        dma((3, batches * SPLIT)),
        dma((3, batches * SPLIT)),
        dma((2, batches * SPLIT)),
        dma((batches,)),
        dma((batches,)),
        pltpu.SemaphoreType.REGULAR,
    ]
    return pl.pallas_call(
        functools.partial(kernel, n_pipe, n_seq, n_mp),
        out_shape=(
            jax.ShapeDtypeStruct((1, batches, toks, share), BF16),
            jax.ShapeDtypeStruct((1, 2, batches, toks, share), BF16),
        ),
        in_specs=[vmem, vmem, vmem, smem, vmem, hbm, hbm, hbm, hbm, vmem],
        out_specs=(vmem, vmem),
        scratch_shapes=scratch,
        compiler_params=pltpu.CompilerParams(
            collective_id=0, has_side_effects=True, vmem_limit_bytes=56 * 1024 * 1024
        ),
    )(enc_in, dec_in, doc_ids, enc_sections, norm_gain, q_weight, k_weight, v_weight, o_weight,
      out_grad)


def solution(mesh):
    sizes = (mesh.shape["pipe"], mesh.shape["seq"], mesh.shape["mp"])
    return jax.shard_map(
        functools.partial(per_device, *sizes),
        mesh=mesh,
        in_specs=(
            P(None, "seq", None),
            P(None, "seq", None),
            P(),
            P(),
            P("pipe", None),
            P("pipe", None, "mp"),
            P("pipe", None, "mp"),
            P("pipe", None, "mp"),
            P("pipe", "mp", None),
            P(None, "seq", None),
        ),
        out_specs=(P("pipe", None, "seq", "mp"), P("pipe", None, None, "seq", "mp")),
        check_vma=False,
    )
```

```python
import functools

import jax
import jax.numpy as jnp
from jax import lax
from jax.experimental import pallas as pl
from jax.experimental.pallas import tpu as pltpu
from jax.sharding import PartitionSpec as P

HEADS = 8
HS = 256
PAD = 128
SPLIT = 2

epsilon = 1e-06
MESH = pl.DeviceIdType.MESH
F32 = jnp.float32
BF16 = jnp.bfloat16


def dot_nn(a, b):
    return jnp.dot(a, b, preferred_element_type=F32)


def dot_nt(a, b):
    return lax.dot_general(a, b, (((1,), (1,)), ((), ())), preferred_element_type=F32)


def dot_tn(a, b):
    return lax.dot_general(a, b, (((0,), (0,)), ((), ())), preferred_element_type=F32)


def kernel(
    n_pipe,
    n_seq,
    n_mp,
    enc_ref,
    dec_ref,
    doc_ref,
    count_ref,
    gain_ref,
    wq_hbm,
    wk_hbm,
    wv_hbm,
    wo_hbm,
    og_ref,
    so_ref,
    sg_ref,
    wq,
    wk,
    wv,
    wo,
    w_sem,
    mask,
    upd_recv,
    enc_recv,
    enc_cur,
    src_cur,
    q_acc,
    k_acc,
    v_acc,
    queries,
    q_factor,
    m_factor,
    q_head,
    k_head,
    kv_all,
    portion,
    attended,
    fs_send,
    fs_recv,
    upd_send,
    u_recv,
    d_att,
    kvg_send,
    kvg_recv,
    q_grad,
    k_grad,
    v_grad,
    dq_buf,
    a_send,
    a_recv,
    b_send,
    b_recv,
    s_send,
    s_recv,
    s_total,
    fs_relay,
    a_relay,
    b_relay,
    ahop,
    bhop,
    gb_recv,
    upd_ssem,
    upd_rsem,
    enc_ssem,
    enc_rsem,
    kv_ssem,
    kv_rsem,
    fs_ssem,
    fs_rsem,
    u_ssem,
    u_rsem,
    kvg_ssem,
    kvg_rsem,
    a_ssem,
    a_rsem,
    b_ssem,
    b_rsem,
    s_ssem,
    s_rsem,
    relay_ssem,
    relay_rsem,
    pass_ssem,
    gb_ssem,
    gb_rsem,
    clear_sem,
):
    pipe = lax.axis_index("pipe")
    seq = lax.axis_index("seq")
    z = lax.axis_index("mp")
    batches, toks, width = enc_ref.shape
    share = width // n_mp
    part = share // SPLIT
    heads = HEADS // n_mp
    units = heads * HS
    scale = HS ** (-0.5)
    last = n_pipe - 1

    def at_mp(j):
        return (pipe, seq, j)

    def at_seq(i):
        return (pipe, i, z)

    def copy(src, dst, ssem, rsem, device):
        return pltpu.make_async_remote_copy(
            src_ref=src,
            dst_ref=dst,
            send_sem=ssem,
            recv_sem=rsem,
            device_id=device,
            device_id_type=MESH,
        )

    weight_loads = [
        pltpu.make_async_copy(hbm.at[0], vmem, w_sem.at[i])
        for i, (hbm, vmem) in enumerate(
            [(wk_hbm, wk), (wv_hbm, wv), (wq_hbm, wq), (wo_hbm, wo)]
        )
    ]
    for load in weight_loads[:2]:
        load.start()

    barrier = pltpu.get_barrier_semaphore()
    for k in range(1, n_mp):
        pl.semaphore_signal(
            barrier, inc=1, device_id=at_mp(lax.rem(z + k, n_mp)), device_id_type=MESH
        )
    for k in range(1, n_seq):
        pl.semaphore_signal(
            barrier, inc=1, device_id=at_seq(lax.rem(seq + k, n_seq)), device_id_type=MESH
        )

    @pl.when(pipe > 0)
    def _():
        for j in range(n_mp):
            pl.semaphore_signal(
                barrier, inc=1, device_id=(pipe - 1, seq, j), device_id_type=MESH
            )

    @pl.when(pipe < last)
    def _():
        for j in range(n_mp):
            pl.semaphore_signal(
                barrier, inc=1, device_id=(pipe + 1, seq, j), device_id_type=MESH
            )

    edge = jnp.where(pipe > 0, n_mp, 0) + jnp.where(pipe < last, n_mp, 0)
    pl.semaphore_wait(barrier, n_mp - 1 + n_seq - 1 + edge)

    for load in weight_loads[2:]:
        load.start()

    encoder = pipe < count_ref[0]
    prev_encoder = pipe - 1 < count_ref[0]

    def span(f, j):
        return pl.ds(pl.multiple_of(j * share + f * part, part), part)

    def cut(ref, m, f, j):
        return ref[m, :, span(f, j)]

    def gain_of(f, j):
        return gain_ref[:, span(f, j)]

    def chunk_rows(ref, f, j):
        return ref[span(f, j), :]

    def chunk_cols(ref, f, j):
        return ref[:, span(f, j)]

    def slabs(m):
        return pl.ds(m * SPLIT, SPLIT)

    pieces = SPLIT * n_mp

    def piece(i):
        return lax.div(i, n_mp), lax.rem(i, n_mp)

    length = n_seq * toks
    for m in range(batches):
        row = doc_ref[m : m + 1, :].astype(F32)
        spread = jnp.broadcast_to(row, (length, length))
        mask[m] = (spread == spread.T).astype(F32)
    eye = (
        lax.broadcasted_iota(jnp.int32, (toks, PAD), 0)
        == lax.broadcasted_iota(jnp.int32, (toks, PAD), 1)
    ).astype(F32)
    my_rows = pl.ds(pl.multiple_of(seq * toks, toks), toks)
    none = jnp.zeros((toks, 1), F32)

    def keys_of(m, h):
        return kv_all[m, :, :, h * HS : (h + 1) * HS].reshape(length, HS)

    def values_of(m, h):
        return kv_all[m, :, :, units + h * HS : units + (h + 1) * HS].reshape(length, HS)

    def enc_copy(m, device):
        return copy(enc_cur.at[slabs(m)], enc_recv.at[slabs(m)], enc_ssem.at[m], enc_rsem.at[m], device)

    def kv_copy(m, slot, peer, owner):
        return copy(
            kv_all.at[m, seq], kv_all.at[m, owner], kv_ssem.at[m, slot], kv_rsem.at[m, owner],
            at_seq(peer),
        )

    def kvg_copy(m, slot, peer, owner):
        return copy(
            kvg_send.at[m, peer], kvg_recv.at[m, owner], kvg_ssem.at[m, slot],
            kvg_rsem.at[m, owner], at_seq(peer),
        )

    def fs_copy(m, j, owner):
        return copy(
            fs_send.at[m, j], fs_recv.at[m, owner], fs_ssem.at[m, j], fs_rsem.at[m, owner],
            at_mp(j),
        )

    def upd_copy(m, j, owner, device):
        return copy(
            upd_send.at[m], upd_recv.at[m, owner], upd_ssem.at[m, j], upd_rsem.at[m, owner],
            device,
        )

    def u_copy(m, j, owner, device):
        return copy(
            ahop.at[m], u_recv.at[m, owner], u_ssem.at[m, j], u_rsem.at[m, owner], device
        )

    def stat_copy(m, j, owner):
        return copy(
            s_send.at[m], s_recv.at[m, owner], s_ssem.at[m, j], s_rsem.at[m, owner], at_mp(j)
        )

    def a_copy(m, j, owner):
        return copy(
            a_send.at[m, j], a_recv.at[m, owner], a_ssem.at[m, j], a_rsem.at[m, owner], at_mp(j)
        )

    def b_copy(m, j, owner):
        return copy(
            b_send.at[m, j], b_recv.at[m, owner], b_ssem.at[m, j], b_rsem.at[m, owner], at_mp(j)
        )

    def gb_copy(m, device):
        return copy(
            bhop.at[slabs(m)], gb_recv.at[slabs(m)], gb_ssem.at[m], gb_rsem.at[m], device
        )

    chain = n_mp == 4
    far = n_mp - 1 - z
    upper = z >= n_mp // 2
    near_z = jnp.where(upper, far, z)
    is_end = near_z == 0 if chain else z < 0
    is_mid = near_z == 1 if chain else z < 0
    partner = jnp.where(upper, n_mp - 2, 1)
    other_end = jnp.where(upper, 0, n_mp - 1)
    this_end = jnp.where(upper, n_mp - 1, 0)

    def mirror(j):
        return jnp.where(upper, n_mp - 1 - j, j)

    def reduce_order(k):
        if not chain:
            return lax.rem(z + 1 + k, n_mp)
        mid = jnp.where(k == 0, 2, jnp.where(k == 3, 3, k - 1))
        return mirror(jnp.where(is_end, 3 - k, mid))

    def gather_order(k):
        if not chain:
            return lax.rem(z + k, n_mp)
        mid = jnp.where(k == 0, 1, jnp.where(k == 1, 3, jnp.where(k == 2, 0, 2)))
        return mirror(jnp.where(is_end, k, mid))

    def skipped(j):
        return jnp.logical_and(is_end, j == far)

    def kept(j):
        return jnp.logical_not(skipped(j))

    def relay_copy(which, m, send, relay):
        return copy(
            send.at[m, far], relay.at[m], relay_ssem.at[which, m], relay_rsem.at[which, m],
            at_mp(partner),
        )

    def pass_copy(which, m, buffer, rsem):
        return copy(
            buffer.at[m, other_end], buffer.at[m, other_end], pass_ssem.at[which, m],
            rsem.at[m, other_end], at_mp(this_end),
        )

    def reduce_part(which, m, k, j, block, send, relay, direct):
        send[m, j] = block.astype(BF16)
        closing = jnp.logical_and(is_mid, k == n_mp - 1)
        opening = jnp.logical_and(is_end, k == 0)

        @pl.when(closing)
        def _():
            relay_copy(which, m, send, relay).wait_recv()
            send[m, j] = (block + relay[m].astype(F32)).astype(BF16)

        @pl.when(opening)
        def _():
            relay_copy(which, m, send, relay).start()

        @pl.when(jnp.logical_and(j != z, kept(j)))
        def _():
            direct(m, j, z).start()

    def reduced(m, send, recv, direct):
        total = send[m, z].astype(F32)
        for k in range(1, n_mp):
            j = lax.rem(z + k, n_mp)

            @pl.when(kept(j))
            def _():
                direct(m, j, j).wait_recv()

            total = total + recv[m, j].astype(F32)
        return total

    def reduce_drain(which, m, send, relay, direct):
        for k in range(1, n_mp):
            j = lax.rem(z + k, n_mp)

            @pl.when(kept(j))
            def _():
                direct(m, j, z).wait_send()

        @pl.when(is_end)
        def _():
            relay_copy(which, m, send, relay).wait_send()

    @pl.when(is_end)
    def _():
        for p in range(batches * SPLIT):
            for recv in (fs_recv, a_recv, b_recv):
                recv[p, far] = jnp.zeros((toks, part), BF16)

    hop_order = [lax.rem(z + k, n_mp) for k in sorted(range(n_mp), key=lambda k: (k == 0, k != 2))]

    def forward_a(m, wait_q):
        @pl.when(pipe == 0)
        def _():
            def fill(i, carry):
                f, j = piece(i)
                upd_recv[m * SPLIT + f, j] = cut(enc_ref, m, f, j)
                return carry

            lax.fori_loop(0, pieces, fill, 0)

        @pl.when(pipe > 1)
        def _():
            enc_copy(m, at_mp(z)).wait_recv()

        k_acc[m] = jnp.zeros((toks, units), F32)
        v_acc[m] = jnp.zeros((toks, units), F32)
        q_acc[m] = jnp.zeros((toks, units), F32)

        def project(i, sums):
            f, k = piece(i)
            j = gather_order(k)
            p = m * SPLIT + f

            @pl.when(pipe > 0)
            def _():
                upd_copy(p, j, j, at_mp(z)).wait_recv()

                @pl.when(jnp.logical_and(is_mid, k == 1))
                def _():
                    pass_copy(0, p, upd_recv, upd_rsem).start()

            fresh = upd_recv[p, j].astype(F32)
            enc = jnp.where(prev_encoder, fresh, enc_recv[p, j].astype(F32))
            dec = jnp.where(prev_encoder, cut(dec_ref, m, f, j).astype(F32), fresh)
            src = jnp.where(encoder, enc, dec)
            enc_cur[p, j] = enc.astype(BF16)
            src_cur[p, j] = src.astype(BF16)
            m_part = (enc * gain_of(f, j)).astype(BF16)
            k_acc[m] += dot_nn(m_part, chunk_rows(wk, f, j))
            v_acc[m] += dot_nn(m_part, chunk_rows(wv, f, j))
            return (
                sums[0] + jnp.sum(src * src, axis=-1, keepdims=True),
                sums[1] + jnp.sum(enc * enc, axis=-1, keepdims=True),
            )

        q_square, m_square = lax.fori_loop(0, pieces, project, (none, none))
        q_factor[m] = lax.rsqrt(q_square / width + epsilon)
        m_factor[m] = lax.rsqrt(m_square / width + epsilon)

        for h in range(heads):
            lanes = slice(h * HS, (h + 1) * HS)
            keys = k_acc[m, :, lanes] * m_factor[m]
            head = lax.rsqrt(jnp.mean(keys * keys, axis=-1, keepdims=True) + epsilon)
            k_head[m, h] = head
            kv_all[m, seq, :, lanes] = (keys * head).astype(BF16)
        kv_all[m, seq, :, units:] = (v_acc[m] * m_factor[m]).astype(BF16)
        for k in range(1, n_seq):
            kv_copy(m, k, lax.rem(seq + k, n_seq), seq).start()

        @pl.when(jnp.logical_and(pipe > 0, pipe < last))
        def _():
            enc_copy(m, (pipe + 1, seq, z)).start()

        if wait_q:
            weight_loads[2].wait()

        def project_q(i, carry):
            f, j = piece(i)
            q_part = (src_cur[m * SPLIT + f, j].astype(F32) * gain_of(f, j)).astype(BF16)
            q_acc[m] += dot_nn(q_part, chunk_rows(wq, f, j))
            return carry

        lax.fori_loop(0, pieces, project_q, 0)
        for h in range(heads):
            lanes = slice(h * HS, (h + 1) * HS)
            found = q_acc[m, :, lanes] * q_factor[m]
            head = lax.rsqrt(jnp.mean(found * found, axis=-1, keepdims=True) + epsilon)
            q_head[m, h] = head
            queries[m, :, lanes] = (found * head).astype(BF16)

    def forward_b(m):
        for k in range(1, n_seq):
            peer = lax.rem(seq + k, n_seq)
            kv_copy(m, k, peer, peer).wait_recv()
        same = mask[m, my_rows, :]
        for h in range(heads):
            lanes = slice(h * HS, (h + 1) * HS)
            scores = dot_nt(queries[m, :, lanes], keys_of(m, h)) * scale
            weights = jnp.exp(scores) * same
            totals = jnp.sum(weights, axis=-1, keepdims=True)
            summed = dot_nn(weights.astype(BF16), values_of(m, h))
            attended[m, :, lanes] = (summed / totals).astype(BF16)
            portion[m, h] = weights / totals

    def forward_out(m):
        def emit(i, carry):
            f, k = piece(i)
            j = reduce_order(k)
            block = dot_nn(attended[m], chunk_cols(wo, f, j))
            reduce_part(0, m * SPLIT + f, k, j, block, fs_send, fs_relay, fs_copy)
            return carry

        lax.fori_loop(0, pieces, emit, 0)

    def forward_c(m):
        for f in range(SPLIT):
            p = m * SPLIT + f
            branch = reduced(p, fs_send, fs_recv, fs_copy)
            updated = (src_cur[p, z].astype(F32) + branch).astype(BF16)
            upd_send[p] = updated

            @pl.when(pipe < last)
            def _():
                for j in hop_order:

                    @pl.when(kept(j))
                    def _():
                        upd_copy(p, j, z, (pipe + 1, seq, j)).start()

            so_ref[0, m, :, f * part : (f + 1) * part] = updated

    def sort_a(dq, dm):
        return jnp.where(encoder, dq + dm, jnp.where(prev_encoder, dm, dq))

    def sort_b(dq, dm):
        return jnp.where(encoder, 0.0, jnp.where(prev_encoder, dq, dm))

    def to_row(column):
        return jnp.sum(column * eye, axis=0, keepdims=True)

    def to_column(row):
        return jnp.sum(row * eye, axis=1, keepdims=True)

    turns = jnp.logical_and(jnp.logical_not(encoder), prev_encoder)
    first = jnp.logical_or(encoder, prev_encoder)

    def backward_pull(m):
        @pl.when(pipe == last)
        def _():
            def fill(i, carry):
                f, j = piece(i)
                start = cut(og_ref, m, f, j).astype(F32)
                u_recv[m * SPLIT + f, j] = jnp.where(encoder, 0.0, start).astype(BF16)
                return carry

            lax.fori_loop(0, pieces, fill, 0)
            for f in range(SPLIT):
                start = cut(og_ref, m, f, z).astype(F32)
                gb_recv[m * SPLIT + f] = jnp.where(encoder, start, 0.0).astype(BF16)

        def pull(i, total):
            f, k = piece(i)
            j = gather_order(k)
            p = m * SPLIT + f

            @pl.when(pipe < last)
            def _():
                u_copy(p, j, j, at_mp(z)).wait_recv()

                @pl.when(jnp.logical_and(is_mid, k == 1))
                def _():
                    pass_copy(1, p, u_recv, u_rsem).start()

            return total + dot_nt(u_recv[p, j], chunk_cols(wo, f, j))

        d_att[m] = lax.fori_loop(
            0, pieces, pull, jnp.zeros((toks, units), F32)).astype(BF16)

    def backward_a(m):
        for h in range(heads):
            lanes = slice(h * HS, (h + 1) * HS)
            wide = slice(units + h * HS, units + (h + 1) * HS)
            probs = portion[m, h]
            pulled = d_att[m, :, lanes]
            along = dot_nt(pulled, values_of(m, h))
            delta = jnp.sum(
                pulled.astype(F32) * attended[m, :, lanes].astype(F32), axis=-1, keepdims=True
            )
            d_scores = (probs * (along - delta)).astype(BF16)
            asked = queries[m, :, lanes]
            value_term = dot_tn(probs.astype(BF16), pulled)
            key_term = dot_tn(d_scores, asked) * scale
            kvg_send[m, :, :, lanes] = key_term.astype(BF16).reshape(n_seq, toks, HS)
            kvg_send[m, :, :, wide] = value_term.astype(BF16).reshape(n_seq, toks, HS)
            d_queries = dot_nn(d_scores, keys_of(m, h)) * scale
            normed = asked.astype(F32)
            mean = jnp.mean(d_queries * normed, axis=-1, keepdims=True)
            q_grad[m, :, lanes] = (q_head[m, h] * (d_queries - normed * mean)).astype(BF16)

        for k in range(1, n_seq):
            kvg_copy(m, k, lax.rem(seq + k, n_seq), seq).start()

        def ask(i, carry):
            f, j = piece(i)
            dq_buf[m * SPLIT + f, j] = dot_nt(q_grad[m], chunk_rows(wq, f, j))
            return carry

        lax.fori_loop(0, pieces, ask, 0)

    def backward_b(m):
        q_stat = jnp.sum(q_grad[m].astype(F32) * q_acc[m], axis=-1, keepdims=True)
        d_kv = kvg_send[m, seq].astype(F32)
        for k in range(1, n_seq):
            peer = lax.rem(seq + k, n_seq)
            kvg_copy(m, k, peer, peer).wait_recv()
            d_kv = d_kv + kvg_recv[m, peer].astype(F32)
        v_grad[m] = d_kv[:, units:].astype(BF16)
        for h in range(heads):
            lanes = slice(h * HS, (h + 1) * HS)
            d_keys = d_kv[:, lanes]
            normed = kv_all[m, seq, :, lanes].astype(F32)
            mean = jnp.mean(d_keys * normed, axis=-1, keepdims=True)
            k_grad[m, :, lanes] = (k_head[m, h] * (d_keys - normed * mean)).astype(BF16)
        m_stat = jnp.sum(
            k_grad[m].astype(F32) * k_acc[m] + v_grad[m].astype(F32) * v_acc[m],
            axis=-1,
            keepdims=True,
        )
        s_send[m, 0:1, :] = to_row(sort_a(q_stat, m_stat))
        s_send[m, 1:2, :] = to_row(sort_b(q_stat, m_stat))
        s_send[m, 2:, :] = jnp.zeros((6, PAD), F32)
        for k in range(1, n_mp):
            stat_copy(m, lax.rem(z + k, n_mp), z).start()

        def spread_out(i, carry):
            f, k = piece(i)
            p = m * SPLIT + f
            j = reduce_order(k)
            dm = dot_nt(k_grad[m], chunk_rows(wk, f, j)) + dot_nt(v_grad[m], chunk_rows(wv, f, j))
            dq = dq_buf[p, j]
            reduce_part(1, p, k, j, sort_a(dq, dm), a_send, a_relay, a_copy)
            b_send[p, j] = sort_b(dq, dm).astype(BF16)
            return carry

        lax.fori_loop(0, pieces, spread_out, 0)

    def norm_back(f, values, factor, total, stat):
        return factor * (gain_of(f, z) * total - values * (factor * factor * (stat / width)))

    def backward_c(m):
        stats = s_send[m]
        for k in range(1, n_mp):
            j = lax.rem(z + k, n_mp)
            stat_copy(m, j, j).wait_recv()
            stats = stats + s_recv[m, j]
        s_total[m] = stats
        factor = jnp.where(turns, m_factor[m], q_factor[m])
        stat = to_column(stats[0:1, :])
        for f in range(SPLIT):
            p = m * SPLIT + f
            total = reduced(p, a_send, a_recv, a_copy)
            if f == 0:

                @pl.when(jnp.logical_and(pipe > 0, pipe < last))
                def _():
                    gb_copy(m, at_mp(z)).wait_recv()

            own = u_recv[p, z].astype(F32)
            ahop[p] = own.astype(BF16)

            @pl.when(pipe > 0)
            def _():
                ahop[p] = jnp.where(turns, gb_recv[p].astype(F32), own).astype(BF16)

            base = ahop[p].astype(F32)
            values = jnp.where(turns, enc_cur[p, z].astype(F32), src_cur[p, z].astype(F32))
            fresh = base + norm_back(f, values, factor, total, stat)
            ahop[p] = fresh.astype(BF16)

            @pl.when(pipe > 0)
            def _():
                for j in hop_order:

                    @pl.when(kept(j))
                    def _():
                        u_copy(p, j, z, (pipe - 1, seq, j)).start()

    def finish(m, f, b_new):
        a_new = ahop[m * SPLIT + f].astype(F32)
        lanes = slice(f * part, (f + 1) * part)
        sg_ref[0, 0, m, :, lanes] = jnp.where(first, a_new, b_new).astype(BF16)
        sg_ref[0, 1, m, :, lanes] = jnp.where(first, b_new, a_new).astype(BF16)

    def backward_d(m):
        @pl.when(pipe == 0)
        def _():
            if last > 0:
                gb_copy(m, at_mp(z)).wait_recv()
            for f in range(SPLIT):
                finish(m, f, gb_recv[m * SPLIT + f].astype(F32))

        @pl.when(pipe > 0)
        def _():
            factor = jnp.where(turns, q_factor[m], m_factor[m])
            stat = to_column(s_total[m, 1:2, :])
            for f in range(SPLIT):
                p = m * SPLIT + f
                total = reduced(p, b_send, b_recv, b_copy)
                base = jnp.where(turns, u_recv[p, z].astype(F32), gb_recv[p].astype(F32))
                values = jnp.where(turns, src_cur[p, z].astype(F32), enc_cur[p, z].astype(F32))
                fresh = base + norm_back(f, values, factor, total, stat)
                bhop[p] = fresh.astype(BF16)
                finish(m, f, fresh)
            gb_copy(m, (pipe - 1, seq, z)).start()

    def backward_rest():
        @pl.when(pipe > 0)
        def _():
            for m in range(batches * SPLIT):
                for j in hop_order:

                    @pl.when(kept(j))
                    def _():
                        u_copy(m, j, z, (pipe - 1, seq, j)).wait_send()

                @pl.when(is_end)
                def _():
                    relay_copy(2, m, b_send, b_relay).start()

                for k in range(1, n_mp):
                    j = lax.rem(z + k, n_mp)
                    held = jnp.logical_and(is_mid, j == other_end)

                    @pl.when(jnp.logical_and(kept(j), jnp.logical_not(held)))
                    def _():
                        b_copy(m, j, z).start()

            @pl.when(is_mid)
            def _():
                for m in range(batches * SPLIT):
                    relay_copy(2, m, b_send, b_relay).wait_recv()
                    joined = b_send[m, other_end].astype(F32) + b_relay[m].astype(F32)
                    b_send[m, other_end] = joined.astype(BF16)
                    b_copy(m, other_end, z).start()

        for m in range(batches):
            backward_d(m)

    @pl.when(pipe < last)
    def _():
        for load in weight_loads[:2]:
            load.wait()
        forward_a(0, True)
        forward_b(0)
        weight_loads[3].wait()
        forward_out(0)
        for m in range(1, batches):
            forward_a(m, False)
            forward_c(m - 1)
            forward_b(m)
            forward_out(m)
        forward_c(batches - 1)
        backward_pull(0)
        backward_a(0)
        backward_b(0)
        for m in range(1, batches):
            backward_pull(m)
            backward_a(m)
            backward_c(m - 1)
            backward_b(m)
        backward_c(batches - 1)
        backward_rest()

        @pl.when(pipe == last - 1)
        def _():
            pl.semaphore_signal(
                clear_sem, inc=1, device_id=(pipe + 1, seq, z), device_id_type=MESH
            )

    @pl.when(pipe == last)
    def _():
        for load in weight_loads:
            load.wait()
        for m in range(batches):
            backward_pull(m)
        forward_a(0, False)
        forward_b(0)
        backward_a(0)
        backward_b(0)
        for m in range(1, batches):
            forward_a(m, False)
            backward_c(m - 1)
            forward_b(m)
            backward_a(m)
            backward_b(m)
        backward_c(batches - 1)
        backward_rest()
        if last > 0:
            pl.semaphore_wait(clear_sem, 1)
        for m in range(batches):
            forward_out(m)
        for m in range(batches):
            forward_c(m)

    @pl.when(jnp.logical_and(pipe > 0, pipe < last))
    def _():
        for m in range(batches):
            enc_copy(m, (pipe + 1, seq, z)).wait_send()

    for m in range(batches):
        for k in range(1, n_seq):
            peer = lax.rem(seq + k, n_seq)
            kv_copy(m, k, peer, seq).wait_send()
            kvg_copy(m, k, peer, seq).wait_send()
        for k in range(1, n_mp):
            stat_copy(m, lax.rem(z + k, n_mp), z).wait_send()
    for p in range(batches * SPLIT):
        reduce_drain(0, p, fs_send, fs_relay, fs_copy)
        reduce_drain(1, p, a_send, a_relay, a_copy)

    @pl.when(pipe < last)
    def _():
        for p in range(batches * SPLIT):
            for j in hop_order:

                @pl.when(kept(j))
                def _():
                    upd_copy(p, j, z, (pipe + 1, seq, j)).wait_send()

            @pl.when(is_mid)
            def _():
                pass_copy(1, p, u_recv, u_rsem).wait_send()

    @pl.when(pipe > 0)
    def _():
        for m in range(batches):
            gb_copy(m, (pipe - 1, seq, z)).wait_send()
        for p in range(batches * SPLIT):
            reduce_drain(2, p, b_send, b_relay, b_copy)

            @pl.when(is_mid)
            def _():
                pass_copy(0, p, upd_recv, upd_rsem).wait_send()


def per_device(n_pipe, n_seq, n_mp, enc_in, dec_in, doc_ids, enc_sections, norm_gain,
               q_weight, k_weight, v_weight, o_weight, out_grad):
    batches, toks, width = enc_in.shape
    share = width // n_mp
    part = share // SPLIT
    heads = HEADS // n_mp
    units = heads * HS
    length = n_seq * toks
    vmem = pl.BlockSpec(memory_space=pltpu.VMEM)
    hbm = pl.BlockSpec(memory_space=pl.ANY)
    smem = pl.BlockSpec(memory_space=pltpu.SMEM)
    V = pltpu.VMEM
    dma = pltpu.SemaphoreType.DMA
    scratch = [
        V((width, units), BF16),
        V((width, units), BF16),
        V((width, units), BF16),
        V((units, width), BF16),
        dma((4,)),
        V((batches, length, length), F32),
        V((batches * SPLIT, n_mp, toks, part), BF16),
        V((batches * SPLIT, n_mp, toks, part), BF16),
        V((batches * SPLIT, n_mp, toks, part), BF16),
        V((batches * SPLIT, n_mp, toks, part), BF16),
        V((batches, toks, units), F32),
        V((batches, toks, units), F32),
        V((batches, toks, units), F32),
        V((batches, toks, units), BF16),
        V((batches, toks, 1), F32),
        V((batches, toks, 1), F32),
        V((batches, heads, toks, 1), F32),
        V((batches, heads, toks, 1), F32),
        V((batches, n_seq, toks, 2 * units), BF16),
        V((batches, heads, toks, length), F32),
        V((batches, toks, units), BF16),
        V((batches * SPLIT, n_mp, toks, part), BF16),
        V((batches * SPLIT, n_mp, toks, part), BF16),
        V((batches * SPLIT, toks, part), BF16),
        V((batches * SPLIT, n_mp, toks, part), BF16),
        V((batches, toks, units), BF16),
        V((batches, n_seq, toks, 2 * units), BF16),
        V((batches, n_seq, toks, 2 * units), BF16),
        V((batches, toks, units), BF16),
        V((batches, toks, units), BF16),
        V((batches, toks, units), BF16),
        V((batches * SPLIT, n_mp, toks, part), F32),
        V((batches * SPLIT, n_mp, toks, part), BF16),
        V((batches * SPLIT, n_mp, toks, part), BF16),
        V((batches * SPLIT, n_mp, toks, part), BF16),
        V((batches * SPLIT, n_mp, toks, part), BF16),
        V((batches, 8, PAD), F32),
        V((batches, n_mp, 8, PAD), F32),
        V((batches, 8, PAD), F32),
        V((batches * SPLIT, toks, part), BF16),
        V((batches * SPLIT, toks, part), BF16),
        V((batches * SPLIT, toks, part), BF16),
        V((batches * SPLIT, toks, part), BF16),
        V((batches * SPLIT, toks, part), BF16),
        V((batches * SPLIT, toks, part), BF16),
        dma((batches * SPLIT, n_mp)),
        dma((batches * SPLIT, n_mp)),
        dma((batches,)),
        dma((batches,)),
        dma((batches, n_seq)),
        dma((batches, n_seq)),
        dma((batches * SPLIT, n_mp)),
        dma((batches * SPLIT, n_mp)),
        dma((batches * SPLIT, n_mp)),
        dma((batches * SPLIT, n_mp)),
        dma((batches, n_seq)),
        dma((batches, n_seq)),
        dma((batches * SPLIT, n_mp)),
        dma((batches * SPLIT, n_mp)),
        dma((batches * SPLIT, n_mp)),
        dma((batches * SPLIT, n_mp)),
        dma((batches, n_mp)),
        dma((batches, n_mp)),
        dma((3, batches * SPLIT)),
        dma((3, batches * SPLIT)),
        dma((2, batches * SPLIT)),
        dma((batches,)),
        dma((batches,)),
        pltpu.SemaphoreType.REGULAR,
    ]
    return pl.pallas_call(
        functools.partial(kernel, n_pipe, n_seq, n_mp),
        out_shape=(
            jax.ShapeDtypeStruct((1, batches, toks, share), BF16),
            jax.ShapeDtypeStruct((1, 2, batches, toks, share), BF16),
        ),
        in_specs=[vmem, vmem, vmem, smem, vmem, hbm, hbm, hbm, hbm, vmem],
        out_specs=(vmem, vmem),
        scratch_shapes=scratch,
        compiler_params=pltpu.CompilerParams(
            collective_id=0, has_side_effects=True, vmem_limit_bytes=56 * 1024 * 1024
        ),
    )(enc_in, dec_in, doc_ids, enc_sections, norm_gain, q_weight, k_weight, v_weight, o_weight,
      out_grad)


def solution(mesh):
    sizes = (mesh.shape["pipe"], mesh.shape["seq"], mesh.shape["mp"])
    return jax.shard_map(
        functools.partial(per_device, *sizes),
        mesh=mesh,
        in_specs=(
            P(None, "seq", None),
            P(None, "seq", None),
            P(),
            P(),
            P("pipe", None),
            P("pipe", None, "mp"),
            P("pipe", None, "mp"),
            P("pipe", None, "mp"),
            P("pipe", "mp", None),
            P(None, "seq", None),
        ),
        out_specs=(P("pipe", None, "seq", "mp"), P("pipe", None, None, "seq", "mp")),
        check_vma=False,
    )
```
